128 devices in a mesh: lon: 16 (over x_lo, y, core), lat: 8 (over x_hi, z).
Axes of the slice: x: 4 (x_hi: 2, x_lo: 2; x = x_hi * 2 + x_lo), y: 4, z: 4, core: 2. Of those that a mesh axis runs over, the one named last changes fastest.
Arguments:
- radiances: bfloat16 [262144, 128], P(('lon', 'lat')), may hold values from -6 to 6
- owner_id: int32 [262144, 1], P(('lon', 'lat')), may hold values from 0 to 127; in each aligned block of 2048 rows (0 to 2047, 2048 to 4095, ...) at most 40 rows name the same one
- cell_index: int32 [262144, 4], P(('lon', 'lat')), may hold values from 0 to 6143
- valid_count: int32 [262144], P(('lon', 'lat')), may hold values from 1 to 4
- row_counts: int32 [128], P(('lon', 'lat')), may hold values from 1024 to 2048, as said below
- jacobian: bfloat16 [128, 96], replicated, may hold values from -0.5 to 0.5
- background: float32 [1536, 512, 96], P('lon', 'lat'), may hold values from -6 to 6
- vertical: float32 [96, 96], replicated, may hold values from -0.625 to 0.625
- lon_kernel: float32 [1536], replicated, may hold values from -0.15625 to 0.15625
Outputs:
- increment: float32 [1536, 512, 96], P('lon', 'lat')
The draws below stay inside these ranges and needn't reach their ends.
Inputs may be any that keep to these rules, and one draw needn't show every extreme that they name: `owner_id`: among the rows of one ingestion list at most 40 name one owner, a bound that some block reaches. `row_counts`: at least half of 2048; some list is full.
All inputs are finite; a program needn't handle non-finite values.
Results may differ from the reference program's by a relative error of at most 0.0011.
Values may be sent and summed in bfloat16 or wider, within the bound.
No kernel may reach another device: no remote copies, remote signals or barrier semaphores. Data moves between devices by JAX's collectives and lax.ppermute only.
A program may use at most 128 MiB of HBM per device.

```python
import math
import jax
import jax.numpy as jnp
import numpy as np
from jax import lax

NLON = 1536
LEV = 96
CH = 128
FOOT = 4
LAT_DEV = 64
R_DEV = 2048
NDEV = 128
LON_DEV = 96
NLAT = 512
R_TOTAL = 262144
CAP = 40
N_LAT = 8


def draw_row_counts(key, part):
    key = jax.random.fold_in(key, 7)
    first_key, second_key = jax.random.split(key)
    counts = jax.random.randint(first_key, (NDEV,), R_DEV // 2, R_DEV + 1)
    chosen = jax.random.randint(second_key, (), 0, NDEV)
    return jnp.where(jnp.arange(NDEV) == chosen, R_DEV, counts).astype(jnp.int32)


def plant(entries, rng, smallest, largest):
    longest = entries.shape.index(max(entries.shape))
    spots = []
    for shift in (0, 1):
        where = [jax.random.randint(jax.random.fold_in(rng, axis), (), 0, length) for axis, length in enumerate(entries.shape)]
        where[longest] = (where[longest] + shift) % entries.shape[longest]
        spots.append(tuple(where))
    return entries.at[spots[0]].set(smallest).at[spots[1]].set(largest)


def levels(own_key, dims, cuts, smallest, high):
    loudness = 1.0
    for dim, parts in cuts:
        heights = jax.random.uniform(jax.random.fold_in(jax.random.fold_in(own_key, 6), dim), (parts,), jnp.float32, smallest / len(cuts), high / len(cuts))
        loudness = loudness * jnp.repeat(jnp.exp(heights), dims[dim] // parts).reshape((-1,) + (1,) * (len(dims) - 1 - dim))
    return loudness


def routed_block(key, own, number, rows, amount, top, bound, slope):
    sequence = jax.random.permutation(key, amount)
    heavy_load, ordinary = shares(amount, rows * top, bound, slope, True), shares(amount, rows * top, bound, slope, False)
    places = jnp.arange(amount)

    def named(tallies, rotation):
        used = int((tallies > 0).sum())
        fixed = max(1, used // 4)
        moved = fixed + (places - fixed + rotation * (used - fixed)) % max(1, amount - fixed)
        return jnp.zeros((amount,), jnp.int32).at[sequence[jnp.where(places < fixed, places, moved)]].set(jnp.asarray(tallies, jnp.int32))

    tallies = jnp.where(number % 4 == 0, named(heavy_load, number // 4), named(ordinary, number - number // 4 - 1))
    mixed = jax.random.permutation(jax.random.fold_in(own, 3), amount)
    source_of, receiver = mixed[0:amount // 2 * 2:2], mixed[1:amount // 2 * 2:2]
    room = jnp.minimum(tallies[source_of] - 1, bound - tallies[receiver]) // 2
    room = jnp.where((source_of == sequence[0]) | (receiver == sequence[0]) | (tallies[receiver] == 0), 0, jnp.maximum(room, 0))
    moved = jax.random.randint(jax.random.fold_in(own, 4), (amount // 2,), 0, 1 << 20) % (room + 1)
    tallies = tallies.at[source_of].add(-moved).at[receiver].add(moved)
    members = jnp.searchsorted(jnp.cumsum(tallies), jnp.arange(rows * top), side="right").astype(jnp.int32)
    table = members.reshape(top, rows).T
    table = table[jax.random.permutation(jax.random.fold_in(own, 1), rows)]
    rotation = jax.random.randint(jax.random.fold_in(own, 2), (rows, 1), 0, top)
    return jnp.take_along_axis(table, (jnp.arange(top)[None, :] + rotation) % top, axis=1)


def shares(number_of, total, most, lean, full):
    loads = [(1 << 20) // math.isqrt(standing ** lean) + 1 for standing in range(1, number_of + 1)]
    largest = most if full else min(most, max(-(-total // number_of), total * loads[0] // sum(loads)))
    least = 1 if total - largest >= number_of - 1 else 0
    holding, rest = [largest] + [least] * (number_of - 1), total - largest - least * (number_of - 1)
    while rest > 0:
        candidates = [i for i in range(1, number_of) if holding[i] < largest] or [i for i in range(1, number_of) if holding[i] < most]
        pool, budget = sum([loads[i] for i in candidates]), rest
        for i in candidates:
            extra = min(most - holding[i], max(1, budget * loads[i] // pool), rest)
            holding[i] = holding[i] + extra
            rest = rest - extra
    return np.array(holding)


def noise(stream_key, extent, scale, bound, pieces=(), kind=jnp.bfloat16):
    gain = levels(stream_key, extent, pieces, -0.22, 0.18) if pieces else 1.0
    values = jax.random.normal(stream_key, extent, jnp.float32) * scale * gain
    return jnp.minimum(jnp.maximum(values, -bound), bound).astype(kind)


def setup_inputs(seed: int = 0) -> dict:
    streams_of = jax.random.split(jax.random.key(seed), 10)
    radiances = noise(streams_of[0], (R_TOTAL, CH), 1.0, 6.0, ((0, 128),))
    owner_id_keys = jax.random.split(jax.random.fold_in(streams_of[1], 1), R_TOTAL // R_DEV)
    owner_id_turns = jax.random.permutation(jax.random.fold_in(streams_of[1], 3), R_TOTAL // R_DEV)
    owner_id = jax.vmap(lambda own, number: routed_block(jax.random.fold_in(streams_of[1], 2), own, number, R_DEV, NDEV, 1, CAP, 2))(owner_id_keys, owner_id_turns).reshape((R_TOTAL, 1))
    cell_index = plant(jax.random.randint(streams_of[2], (R_TOTAL, FOOT), 0, LON_DEV * LAT_DEV), jax.random.fold_in(streams_of[2], 1), 0, (LON_DEV * LAT_DEV) - 1).astype(jnp.int32)
    valid_count = plant(jax.random.randint(streams_of[3], (R_TOTAL,), 1, FOOT + 1), jax.random.fold_in(streams_of[3], 1), 1, FOOT).astype(jnp.int32)
    row_counts = draw_row_counts(jax.random.fold_in(streams_of[9], 71), 0)
    jacobian = noise(streams_of[5], (CH, LEV), CH ** -0.5, 0.5)
    background = noise(streams_of[6], (NLON, NLAT, LEV), 1.0, 6.0, ((0, 16), (1, 8)), jnp.float32)
    vertical = noise(streams_of[7], (LEV, LEV), LEV ** -0.5, 0.625, (), jnp.float32)
    lon_kernel = noise(streams_of[8], (NLON,), NLON ** -0.5, 0.15625, (), jnp.float32)
    return dict(radiances=radiances, owner_id=owner_id, cell_index=cell_index, valid_count=valid_count, row_counts=row_counts, jacobian=jacobian, background=background, vertical=vertical, lon_kernel=lon_kernel)


def reference(radiances, owner_id, cell_index, valid_count, row_counts, jacobian, background, vertical, lon_kernel):
    position = jnp.arange(R_TOTAL, dtype=jnp.int32)
    is_live = (position % R_DEV) < row_counts[position // R_DEV]
    profile = jnp.dot(radiances, jacobian, preferred_element_type=jnp.float32)
    share = (profile * (1.0 / valid_count.astype(jnp.float32))[:, None]).astype(jnp.bfloat16)
    share = lax.optimization_barrier(share).astype(jnp.float32)
    live_weight = jnp.where(is_live, jnp.ones((R_TOTAL,), jnp.float32), jnp.zeros((R_TOTAL,), jnp.float32))
    owners = owner_id[:, 0]
    sector = owners // N_LAT
    band = owners % N_LAT
    forcing = jnp.zeros((NLON * NLAT, LEV), jnp.float32)
    for slot_number in range(FOOT):
        cell = cell_index[:, slot_number]
        lon_pos = sector * LON_DEV + cell // LAT_DEV
        lat_pos = band * LAT_DEV + cell % LAT_DEV
        used = jnp.where(slot_number < valid_count, live_weight, jnp.zeros_like(live_weight))
        forcing = forcing.at[lon_pos * NLAT + lat_pos].add(share * used[:, None])
    total = background.reshape(NLON * NLAT, LEV) + forcing
    mixed = jnp.dot(total, vertical.T, precision=lax.Precision.HIGHEST, preferred_element_type=jnp.float32)
    mixed = mixed.reshape(NLON, NLAT, LEV)
    spectrum = jnp.fft.rfft(lon_kernel)
    result = jnp.fft.irfft(jnp.fft.rfft(mixed, axis=0) * spectrum[:, None, None], n=NLON, axis=0)
    return result.astype(jnp.float32)
```

```python
import jax
import jax.numpy as jnp
from jax import lax
from jax.experimental import pallas as pl
from jax.experimental.pallas import tpu as pltpu
from jax.sharding import PartitionSpec as P

F32 = jnp.float32
BF16 = jnp.bfloat16
I32 = jnp.int32
I16 = jnp.int16
LANES = 128
TOP = 32700.0
LOWEST = -110.0
CODE_ROWS = 8


def vmem(n):
    return [pl.BlockSpec(memory_space=pltpu.VMEM)] * n


def params():
    return pltpu.CompilerParams(vmem_limit_bytes=56 * 1024 * 1024)


def quantise(tiles, out_ref, place):
    rows = tiles[0].shape[0]
    for k, tile in enumerate(tiles):
        top = jnp.max(jnp.abs(tile), axis=0, keepdims=True)
        power = jnp.maximum(jnp.ceil(jnp.log2(top)), LOWEST)
        factor = jnp.exp2(-power) * TOP
        digits = jnp.round(tile * factor)
        codes = jnp.broadcast_to(power, (CODE_ROWS, LANES))
        whole = jnp.concatenate([digits, codes], axis=0).astype(I32)
        out_ref[place, :, k * LANES : (k + 1) * LANES] = whole.astype(I16)


def dequantise(in_ref, place):
    whole = in_ref[place].astype(I32).astype(F32)
    rows = whole.shape[0] - CODE_ROWS
    factor = jnp.exp2(whole[rows : rows + 1]) * (1.0 / TOP)
    return whole[:rows] * factor


def split(x):
    high = x.astype(BF16)
    low = (x - high.astype(F32)).astype(BF16)
    return high, low


def dispatch_kernel(
    capacity,
    live_ref,
    rad_ref,
    owner_ref,
    cell_ref,
    count_ref,
    jac_ref,
    out_ref,
    pay_ref,
    rows_ref,
    slot_v,
    slot_s,
    sem,
):
    nrows = rad_ref.shape[0]
    levels = jac_ref.shape[0]
    slots = out_ref.shape[0]
    ndev = slots // capacity
    foot = cell_ref.shape[0]
    n_live = live_ref[0]
    block = 256
    owner_ids = lax.broadcasted_iota(I32, (ndev, block), 0)
    earlier = (
        lax.broadcasted_iota(I32, (block, block), 0) < lax.broadcasted_iota(I32, (block, block), 1)
    ).astype(F32).astype(BF16)
    carry = jnp.zeros((ndev, 1), F32)
    for b in range(nrows // block):
        cols = slice(b * block, (b + 1) * block)
        position = lax.broadcasted_iota(I32, (1, block), 1) + b * block
        live = position < n_live
        owner = owner_ref[:, cols]
        hit = ((owner_ids == owner) & live).astype(F32)
        before = jnp.dot(hit.astype(BF16), earlier, preferred_element_type=F32) + carry
        rank = jnp.sum(hit * before, axis=0, keepdims=True).astype(I32)
        carry = carry + jnp.sum(hit, axis=1, keepdims=True)
        slot = jnp.where(live, owner * capacity + rank, slots)
        for i in range(block // LANES):
            row = b * (block // LANES) + i
            slot_v[row : row + 1, :] = slot[:, i * LANES : (i + 1) * LANES]
    copy = pltpu.make_async_copy(slot_v, slot_s, sem)
    copy.start()
    for b in range(nrows // block):
        cols = slice(b * block, (b + 1) * block)
        profile = lax.dot_general(
            jac_ref[...], rad_ref[cols, :], (((1,), (1,)), ((), ())), preferred_element_type=F32
        )
        count = count_ref[:, cols]
        share = (profile * (1.0 / count.astype(F32))).astype(BF16).astype(F32)
        cell = cell_ref[:, cols]
        used = lax.broadcasted_iota(I32, (foot, block), 0) < count
        lon = jnp.where(used, cell // 64, 0).astype(F32)
        lat = jnp.where(used, cell % 64, 64).astype(F32)
        rest = jnp.where(
            lax.broadcasted_iota(I32, (LANES - levels - 2 * foot, block), 0) == 0, 1.0, 0.0
        )
        payload = jnp.concatenate([share, jnp.concatenate([lon, lat], axis=0), rest], axis=0)
        pay_ref[cols, :] = payload.T
    rows_ref[...] = jnp.zeros_like(rows_ref)
    copy.wait()
    unroll = 16

    def move(c, _):
        for u in range(unroll):
            slot = slot_s[c // (LANES // unroll), (c % (LANES // unroll)) * unroll + u]
            rows_ref[pl.ds(slot, 1), :] = pay_ref[pl.ds(c * unroll + u, 1), :]
        return 0

    lax.fori_loop(0, (n_live + unroll - 1) // unroll, move, 0)
    out_ref[...] = rows_ref[:slots, :].astype(BF16)


def spread_kernel(
    capacity,
    lon_dev,
    lat_dev,
    got_ref,
    back_ref,
    vert_ref,
    out_ref,
    mix_ref,
    share_ref,
    acc0,
    acc1,
    acc2,
    acc3,
    meta_v,
    meta_s,
    sem,
):
    slots = got_ref.shape[0]
    levels = back_ref.shape[1]
    ndev = slots // capacity
    ncells = lon_dev * lat_dev
    foot = 4
    row_i = lax.broadcasted_iota(I32, (8, LANES), 0)
    lane_i = lax.broadcasted_iota(I32, (8, LANES), 1)
    is_foot = row_i < foot
    pick = jnp.where(is_foot & (lane_i == levels + row_i), 1.0, 0.0)
    pick = pick + jnp.where(is_foot & (lane_i == levels + foot + row_i), float(lon_dev), 0.0)
    pick = pick + jnp.where((row_i == foot) & (lane_i == levels + 2 * foot), 1.0, 0.0)
    pick = pick.astype(BF16)
    block = 512
    for b in range(slots // block):
        rows = slice(b * block, (b + 1) * block)
        part = got_ref[rows, :]
        meta = lax.dot_general(pick, part, (((1,), (1,)), ((), ())), preferred_element_type=F32)
        meta_v[:, rows] = meta.astype(I32)
        share_ref[rows, :] = part.astype(F32)
    copy = pltpu.make_async_copy(meta_v, meta_s, sem)
    copy.start()
    v_high, v_low = split(vert_ref[...])
    mix_ref[...] = jnp.zeros_like(mix_ref)
    mix_ref[:levels, :levels] = v_high
    mix_ref[:levels, LANES : LANES + levels] = v_high
    mix_ref[LANES : LANES + levels, :levels] = v_low
    for lat in range(lat_dev):
        acc0[lat * lon_dev : (lat + 1) * lon_dev, :levels] = back_ref[
            pl.ds(lat, lon_dev, stride=lat_dev), :
        ]
    accs = (acc0, acc1, acc2, acc3)
    for acc in accs[1:]:
        acc[...] = jnp.zeros_like(acc)
    copy.wait()
    chunk = 8

    def one_source(s, _):
        base = s * capacity
        n_chunks = meta_s[foot, base]
        for c in range(1, capacity // chunk):
            n_chunks = n_chunks + meta_s[foot, base + c * chunk]

        def one_chunk(c, _):
            first = base + c * chunk
            for u in range(chunk):
                row = share_ref[pl.ds(first + u, 1), :]
                for f in range(foot):
                    cell = meta_s[f, first + u]
                    accs[f][pl.ds(cell, 1), :] = accs[f][pl.ds(cell, 1), :] + row
            return 0

        lax.fori_loop(0, n_chunks, one_chunk, 0)
        return 0

    lax.fori_loop(0, ndev, one_source, 0)
    lane = lax.broadcasted_iota(I32, (lon_dev, LANES), 1)
    real = lax.broadcasted_iota(I32, (4 * lon_dev, LANES), 1) < levels

    def one_group(t, _):
        rows = pl.ds(pl.multiple_of(t * 4 * lon_dev, 4 * lon_dev), 4 * lon_dev)
        total = (acc0[rows, :] + acc1[rows, :]) + (acc2[rows, :] + acc3[rows, :])
        total = jnp.where(real, total, 0.0)
        high, low = split(total)
        both = lax.dot_general(
            jnp.concatenate([high, low], axis=1),
            mix_ref[...],
            (((1,), (1,)), ((), ())),
            preferred_element_type=F32,
        )
        mixed = both[:, :LANES] + both[:, LANES:]
        a = [mixed[j * lon_dev : (j + 1) * lon_dev, :] for j in range(4)]
        r1 = pltpu.roll(a[1], 96, 1)
        r2 = pltpu.roll(a[2], 64, 1)
        r3 = pltpu.roll(a[3], 32, 1)
        tiles = [
            jnp.where(lane < 96, a[0], r1),
            jnp.where(lane < 64, r1, r2),
            jnp.where(lane < 32, r2, r3),
        ]
        quantise(tiles, out_ref, t)
        return 0

    lax.fori_loop(0, ncells // (4 * lon_dev), one_group, 0)


def toeplitz_kernel(kern_ref, ph_ref, pl_ref, mh_ref, ml_ref):
    n = kern_ref.shape[1]
    block = 256
    for high_ref, low_ref, row, sign in ((ph_ref, pl_ref, 0, False), (mh_ref, ml_ref, 1, True)):
        base = jnp.broadcast_to(kern_ref[row : row + 1, :], (block, n))
        strip = pltpu.roll(base, 0, 1, stride=1, stride_axis=0)
        for i in range(n // block):
            if i:
                strip = jnp.concatenate([strip[:, n - block :], strip[:, : n - block]], axis=1)
            piece = strip
            if sign:
                row_i = lax.broadcasted_iota(I32, (block, n), 0) + i * block
                piece = jnp.where(lax.broadcasted_iota(I32, (block, n), 1) > row_i, -strip, strip)
            high, low = split(piece)
            high_ref[i * block : (i + 1) * block, :] = high
            low_ref[i * block : (i + 1) * block, :] = low


def conv_kernel(got_ref, ph_ref, pl_ref, mh_ref, ml_ref, out_ref, xph, xpl, xmh, xml, yp, ym):
    n_lon = got_ref.shape[0]
    rows = got_ref.shape[1] - CODE_ROWS
    half = n_lon // 2
    for s in range(half):
        a = dequantise(got_ref, s)
        b = dequantise(got_ref, s + half)
        at = slice(s * rows, (s + 1) * rows)
        xph[at, :], xpl[at, :] = split(a + b)
        xmh[at, :], xml[at, :] = split(a - b)
    for th, tl, xh, xl, y in ((ph_ref, pl_ref, xph, xpl, yp), (mh_ref, ml_ref, xmh, xml, ym)):
        y[...] = (
            jnp.dot(th[...], xh[...], preferred_element_type=F32)
            + jnp.dot(tl[...], xh[...], preferred_element_type=F32)
            + jnp.dot(th[...], xl[...], preferred_element_type=F32)
        )
    width = got_ref.shape[2]
    for s in range(half):
        at = slice(s * rows, (s + 1) * rows)
        plus, minus = yp[at, :], ym[at, :]
        for place, y in ((s, 0.5 * (plus + minus)), (s + half, 0.5 * (plus - minus))):
            quantise([y[:, k : k + LANES] for k in range(0, width, LANES)], out_ref, place)


def unpack_kernel(lat_dev, got_ref, out_ref):
    n_lon = got_ref.shape[0]
    lon_dev = got_ref.shape[1] - CODE_ROWS
    levels = out_ref.shape[1]
    lane = lax.broadcasted_iota(I32, (lon_dev, LANES), 1)
    for t in range(n_lon):
        x = dequantise(got_ref, t)
        o = [x[:, k * LANES : (k + 1) * LANES] for k in range(3)]
        a = [
            o[0],
            pltpu.roll(jnp.where(lane >= 96, o[0], o[1]), 32, 1),
            pltpu.roll(jnp.where(lane >= 64, o[1], o[2]), 64, 1),
            pltpu.roll(o[2], 96, 1),
        ]
        for j in range(4):
            out_ref[pl.ds(t * 4 + j, lon_dev, stride=lat_dev), :] = a[j][:, :levels]


def per_device(
    radiances,
    owner_id,
    cell_index,
    valid_count,
    row_counts,
    jacobian,
    background,
    vertical,
    lon_kernel,
):
    n_lon = lax.axis_size("lon")
    ndev = n_lon * lax.axis_size("lat")
    nrows = radiances.shape[0]
    lon_dev, lat_dev, levels = background.shape
    capacity = 5 * nrows // (2 * ndev)
    slots = ndev * capacity
    ncells = lon_dev * lat_dev
    width = ncells // n_lon // lon_dev * levels
    coded = (n_lon, lon_dev + CODE_ROWS, width)

    sent = pl.pallas_call(
        lambda *refs: dispatch_kernel(capacity, *refs),
        out_shape=jax.ShapeDtypeStruct((slots, LANES), BF16),
        in_specs=[pl.BlockSpec(memory_space=pltpu.SMEM)] + vmem(5),
        out_specs=vmem(1)[0],
        scratch_shapes=[
            pltpu.VMEM((nrows, LANES), F32),
            pltpu.VMEM((slots + 8, LANES), F32),
            pltpu.VMEM((nrows // LANES, LANES), I32),
            pltpu.SMEM((nrows // LANES, LANES), I32),
            pltpu.SemaphoreType.DMA,
        ],
        compiler_params=params(),
        name="dispatch",
    )(
        row_counts,
        radiances,
        owner_id.T,
        cell_index.T,
        valid_count.reshape(1, nrows),
        jacobian.T,
    )
    got = lax.all_to_all(
        sent.reshape(ndev, capacity, LANES), ("lon", "lat"), split_axis=0, concat_axis=0, tiled=True
    ).reshape(slots, LANES)

    acc = pltpu.VMEM((ncells + 8, LANES), F32)
    field = pl.pallas_call(
        lambda *refs: spread_kernel(capacity, lon_dev, lat_dev, *refs),
        out_shape=jax.ShapeDtypeStruct(coded, I16),
        in_specs=vmem(3),
        out_specs=vmem(1)[0],
        scratch_shapes=[
            pltpu.VMEM((2 * LANES, 2 * LANES), BF16),
            pltpu.VMEM((slots, LANES), F32),
            acc,
            acc,
            acc,
            acc,
            pltpu.VMEM((8, slots), I32),
            pltpu.SMEM((8, slots), I32),
            pltpu.SemaphoreType.DMA,
        ],
        compiler_params=params(),
        name="spread",
    )(got, background.reshape(ncells, levels), vertical)

    half = n_lon * lon_dev // 2
    turned_kernel = jnp.roll(lon_kernel[::-1], 1)
    plus = turned_kernel[:half] + turned_kernel[half:]
    minus = turned_kernel[half:] - turned_kernel[:half]
    first = lon_kernel[:half] - lon_kernel[half:]
    minus = jnp.roll(first[::-1], 1)
    square = jax.ShapeDtypeStruct((half, half), BF16)
    toeplitz = pl.pallas_call(
        toeplitz_kernel,
        out_shape=(square,) * 4,
        in_specs=vmem(1),
        out_specs=tuple(vmem(4)),
        compiler_params=params(),
        name="toeplitz",
    )(jnp.stack([plus, minus]))

    columns = lax.all_to_all(field, "lon", split_axis=0, concat_axis=0, tiled=True)
    part = pltpu.VMEM((half, width), BF16)
    wide = pltpu.VMEM((half, width), F32)
    result = pl.pallas_call(
        conv_kernel,
        out_shape=jax.ShapeDtypeStruct(coded, I16),
        in_specs=vmem(5),
        out_specs=vmem(1)[0],
        scratch_shapes=[part, part, part, part, wide, wide],
        compiler_params=params(),
        name="convolve",
    )(columns, *toeplitz)
    back = lax.all_to_all(result, "lon", split_axis=0, concat_axis=0, tiled=True)
    out = pl.pallas_call(
        lambda *refs: unpack_kernel(lat_dev, *refs),
        out_shape=jax.ShapeDtypeStruct((ncells, levels), F32),
        in_specs=vmem(1),
        out_specs=vmem(1)[0],
        compiler_params=params(),
        name="unpack",
    )(back)
    return out.reshape(lon_dev, lat_dev, levels)


def solution(mesh):
    return jax.shard_map(
        per_device,
        mesh=mesh,
        in_specs=(
            P(("lon", "lat"), None),
            P(("lon", "lat"), None),
            P(("lon", "lat"), None),
            P(("lon", "lat")),
            P(("lon", "lat")),
            P(),
            P("lon", "lat", None),
            P(),
            P(),
        ),
        out_specs=P("lon", "lat", None),
        check_vma=False,
    )
```

```python
import jax
import jax.numpy as jnp
from jax import lax
from jax.experimental import pallas as pl
from jax.experimental.pallas import tpu as pltpu
from jax.sharding import PartitionSpec as P

F32 = jnp.float32
BF16 = jnp.bfloat16
I32 = jnp.int32
I16 = jnp.int16
LANES = 128
TOP = 32700.0
LOWEST = -110.0
CODE_ROWS = 8


def vmem(n):
    return [pl.BlockSpec(memory_space=pltpu.VMEM)] * n


def params():
    return pltpu.CompilerParams(vmem_limit_bytes=56 * 1024 * 1024)


def quantise(tiles, out_ref, place):
    rows = tiles[0].shape[0]
    for k, tile in enumerate(tiles):
        top = jnp.max(jnp.abs(tile), axis=0, keepdims=True)
        power = jnp.maximum(jnp.ceil(jnp.log2(top)), LOWEST)
        factor = jnp.exp2(-power) * TOP
        digits = jnp.round(tile * factor)
        codes = jnp.broadcast_to(power, (CODE_ROWS, LANES))
        whole = jnp.concatenate([digits, codes], axis=0).astype(I32)
        out_ref[place, :, k * LANES : (k + 1) * LANES] = whole.astype(I16)


def dequantise(in_ref, place):
    whole = in_ref[place].astype(I32).astype(F32)
    rows = whole.shape[0] - CODE_ROWS
    factor = jnp.exp2(whole[rows : rows + 1]) * (1.0 / TOP)
    return whole[:rows] * factor


def split(x):
    high = x.astype(BF16)
    low = (x - high.astype(F32)).astype(BF16)
    return high, low


def dispatch_kernel(
    capacity,
    live_ref,
    rad_ref,
    owner_ref,
    cell_ref,
    count_ref,
    jac_ref,
    out_ref,
    pay_ref,
    even_ref,
    odd_ref,
    slot_v,
    slot_s,
    sem,
):
    nrows = rad_ref.shape[0]
    levels = jac_ref.shape[0]
    slots = out_ref.shape[0]
    ndev = slots // capacity
    foot = cell_ref.shape[0]
    n_live = live_ref[0]
    block = 256
    owner_ids = lax.broadcasted_iota(I32, (ndev, block), 0)
    earlier = (
        lax.broadcasted_iota(I32, (block, block), 0) < lax.broadcasted_iota(I32, (block, block), 1)
    ).astype(F32).astype(BF16)
    carry = jnp.zeros((ndev, 1), F32)
    for b in range(nrows // block):
        cols = slice(b * block, (b + 1) * block)
        position = lax.broadcasted_iota(I32, (1, block), 1) + b * block
        live = position < n_live
        owner = owner_ref[:, cols]
        hit = ((owner_ids == owner) & live).astype(F32)
        before = jnp.dot(hit.astype(BF16), earlier, preferred_element_type=F32) + carry
        rank = jnp.sum(hit * before, axis=0, keepdims=True).astype(I32)
        carry = carry + jnp.sum(hit, axis=1, keepdims=True)
        slot = jnp.where(live, owner * capacity + rank, slots)
        for i in range(block // LANES):
            row = b * (block // LANES) + i
            slot_v[row : row + 1, :] = slot[:, i * LANES : (i + 1) * LANES]
    copy = pltpu.make_async_copy(slot_v, slot_s, sem)
    copy.start()
    for b in range(nrows // block):
        cols = slice(b * block, (b + 1) * block)
        profile = lax.dot_general(
            jac_ref[...], rad_ref[cols, :], (((1,), (1,)), ((), ())), preferred_element_type=F32
        )
        count = count_ref[:, cols]
        share = (profile * (1.0 / count.astype(F32))).astype(BF16).astype(F32)
        cell = cell_ref[:, cols]
        used = lax.broadcasted_iota(I32, (foot, block), 0) < count
        lon = jnp.where(used, cell // 64, 0).astype(F32)
        lat = jnp.where(used, cell % 64, 64).astype(F32)
        rest = jnp.where(
            lax.broadcasted_iota(I32, (LANES - levels - 2 * foot, block), 0) == 0, 1.0, 0.0
        )
        payload = jnp.concatenate([share, jnp.concatenate([lon, lat], axis=0), rest], axis=0)
        pay_ref[cols, :] = payload.T
    even_ref[...] = jnp.zeros_like(even_ref)
    odd_ref[...] = jnp.zeros_like(odd_ref)
    copy.wait()
    unroll = 16

    def move(c, _):
        for u in range(unroll):
            slot = slot_s[c // (LANES // unroll), (c % (LANES // unroll)) * unroll + u]
            to_ref = odd_ref if u % 2 else even_ref
            to_ref[pl.ds(slot, 1), :] = pay_ref[pl.ds(c * unroll + u, 1), :]
        return 0

    lax.fori_loop(0, (n_live + unroll - 1) // unroll, move, 0)
    out_ref[...] = (even_ref[:slots, :] + odd_ref[:slots, :]).astype(BF16)


def spread_kernel(
    capacity,
    lon_dev,
    lat_dev,
    levels,
    got_ref,
    back_ref,
    mix_ref,
    out_ref,
    share_ref,
    acc0,
    acc1,
    acc2,
    acc3,
    meta_v,
    meta_s,
    sems,
):
    slots = got_ref.shape[0]
    ndev = slots // capacity
    ncells = lon_dev * lat_dev
    foot = 4
    load = pltpu.make_async_copy(back_ref, acc0.at[pl.ds(0, ncells), :], sems.at[0])
    load.start()
    row_i = lax.broadcasted_iota(I32, (8, LANES), 0)
    lane_i = lax.broadcasted_iota(I32, (8, LANES), 1)
    is_foot = row_i < foot
    pick = jnp.where(is_foot & (lane_i == levels + row_i), 1.0, 0.0)
    pick = pick + jnp.where(is_foot & (lane_i == levels + foot + row_i), float(lon_dev), 0.0)
    pick = pick + jnp.where((row_i == foot) & (lane_i == levels + 2 * foot), 1.0, 0.0)
    pick = pick.astype(BF16)
    block = 512
    for b in range(slots // block):
        rows = slice(b * block, (b + 1) * block)
        part = got_ref[rows, :]
        meta = lax.dot_general(pick, part, (((1,), (1,)), ((), ())), preferred_element_type=F32)
        meta_v[:, rows] = meta.astype(I32)
        share_ref[rows, :] = part.astype(F32)
    copy = pltpu.make_async_copy(meta_v, meta_s, sems.at[1])
    copy.start()
    accs = (acc0, acc1, acc2, acc3)
    for acc in accs[1:]:
        acc[...] = jnp.zeros_like(acc)
    load.wait()
    copy.wait()
    chunk = 8

    def one_source(s, _):
        base = s * capacity
        n_chunks = meta_s[foot, base]
        for c in range(1, capacity // chunk):
            n_chunks = n_chunks + meta_s[foot, base + c * chunk]

        def one_chunk(c, _):
            first = base + c * chunk
            for u in range(chunk):
                row = share_ref[pl.ds(first + u, 1), :]
                for f in range(foot):
                    cell = meta_s[f, first + u]
                    accs[f][pl.ds(cell, 1), :] = accs[f][pl.ds(cell, 1), :] + row
            return 0

        lax.fori_loop(0, n_chunks, one_chunk, 0)
        return 0

    lax.fori_loop(0, ndev, one_source, 0)
    lane = lax.broadcasted_iota(I32, (lon_dev, LANES), 1)

    def one_group(t, _):
        rows = pl.ds(pl.multiple_of(t * 4 * lon_dev, 4 * lon_dev), 4 * lon_dev)
        total = (acc0[rows, :] + acc1[rows, :]) + (acc2[rows, :] + acc3[rows, :])
        high, low = split(total)
        both = jnp.dot(
            jnp.concatenate([high, low], axis=1), mix_ref[...], preferred_element_type=F32
        )
        mixed = both[:, :LANES] + both[:, LANES:]
        a = [mixed[j * lon_dev : (j + 1) * lon_dev, :] for j in range(4)]
        r1 = pltpu.roll(a[1], 96, 1)
        r2 = pltpu.roll(a[2], 64, 1)
        r3 = pltpu.roll(a[3], 32, 1)
        tiles = [
            jnp.where(lane < 96, a[0], r1),
            jnp.where(lane < 64, r1, r2),
            jnp.where(lane < 32, r2, r3),
        ]
        quantise(tiles, out_ref, t)
        return 0

    lax.fori_loop(0, ncells // (4 * lon_dev), one_group, 0, unroll=4)


def prepare_kernel(lat_dev, back_ref, vert_ref, out_ref, mix_ref):
    ncells, levels = back_ref.shape
    lon_dev = ncells // lat_dev
    v_high, v_low = split(vert_ref[...])
    mix_ref[...] = jnp.zeros_like(mix_ref)
    mix_ref[:levels, :levels] = v_high
    mix_ref[:levels, LANES : LANES + levels] = v_low
    mix_ref[LANES : LANES + levels, :levels] = v_high
    out_ref[...] = jnp.zeros_like(out_ref)
    for lat in range(lat_dev):
        out_ref[lat * lon_dev : (lat + 1) * lon_dev, :levels] = back_ref[
            pl.ds(lat, lon_dev, stride=lat_dev), :
        ]


def toeplitz_kernel(kern_ref, ph_ref, pl_ref, mh_ref, ml_ref):
    n = kern_ref.shape[1]
    block = 256
    for high_ref, low_ref, row, sign in ((ph_ref, pl_ref, 0, False), (mh_ref, ml_ref, 1, True)):
        base = jnp.broadcast_to(kern_ref[row : row + 1, :], (block, n))
        strip = pltpu.roll(base, 0, 1, stride=1, stride_axis=0)
        for i in range(n // block):
            if i:
                strip = jnp.concatenate([strip[:, n - block :], strip[:, : n - block]], axis=1)
            piece = strip
            if sign:
                row_i = lax.broadcasted_iota(I32, (block, n), 0) + i * block
                piece = jnp.where(lax.broadcasted_iota(I32, (block, n), 1) > row_i, -strip, strip)
            high, low = split(piece)
            high_ref[i * block : (i + 1) * block, :] = high
            low_ref[i * block : (i + 1) * block, :] = low


def conv_kernel(got_ref, *refs):
    hbm, out_ref, held, (xph, xpl, xmh, xml, yp, ym, sems) = refs[:4], refs[4], refs[5:9], refs[9:]
    loads = [pltpu.make_async_copy(a, b, sems.at[i]) for i, (a, b) in enumerate(zip(hbm, held))]
    for load in loads:
        load.start()
    ph_ref, pl_ref, mh_ref, ml_ref = held
    n_lon = got_ref.shape[0]
    rows = got_ref.shape[1] - CODE_ROWS
    half = n_lon // 2
    for s in range(half):
        a = dequantise(got_ref, s)
        b = dequantise(got_ref, s + half)
        at = slice(s * rows, (s + 1) * rows)
        xph[at, :], xpl[at, :] = split(a + b)
        xmh[at, :], xml[at, :] = split(a - b)
    for load in loads:
        load.wait()
    for th, tl, xh, xl, y in ((ph_ref, pl_ref, xph, xpl, yp), (mh_ref, ml_ref, xmh, xml, ym)):
        y[...] = (
            jnp.dot(th[...], xh[...], preferred_element_type=F32)
            + jnp.dot(tl[...], xh[...], preferred_element_type=F32)
            + jnp.dot(th[...], xl[...], preferred_element_type=F32)
        )
    width = got_ref.shape[2]
    for s in range(half):
        at = slice(s * rows, (s + 1) * rows)
        plus, minus = yp[at, :], ym[at, :]
        for place, y in ((s, 0.5 * (plus + minus)), (s + half, 0.5 * (plus - minus))):
            quantise([y[:, k : k + LANES] for k in range(0, width, LANES)], out_ref, place)


def unpack_kernel(got_ref, out_ref):
    lon_dev, lats, levels = out_ref.shape
    lane = lax.broadcasted_iota(I32, (lon_dev, LANES), 1)
    flat = out_ref.reshape(lon_dev * lats, levels)
    for t in range(got_ref.shape[0]):
        x = dequantise(got_ref, t)
        o = [x[:, k * LANES : (k + 1) * LANES] for k in range(3)]
        a = [
            o[0],
            pltpu.roll(jnp.where(lane >= 96, o[0], o[1]), 32, 1),
            pltpu.roll(jnp.where(lane >= 64, o[1], o[2]), 64, 1),
            pltpu.roll(o[2], 96, 1),
        ]
        for j in range(4):
            flat[pl.ds(t * 4 + j, lon_dev, stride=lats), :] = a[j][:, :levels]


def per_device(
    radiances,
    owner_id,
    cell_index,
    valid_count,
    row_counts,
    jacobian,
    background,
    vertical,
    lon_kernel,
):
    n_lon = lax.axis_size("lon")
    ndev = n_lon * lax.axis_size("lat")
    nrows = radiances.shape[0]
    lon_dev, lat_dev, levels = background.shape
    capacity = 5 * nrows // (2 * ndev)
    slots = ndev * capacity
    ncells = lon_dev * lat_dev
    width = ncells // n_lon // lon_dev * levels
    coded = (n_lon, lon_dev + CODE_ROWS, width)

    sent = pl.pallas_call(
        lambda *refs: dispatch_kernel(capacity, *refs),
        out_shape=jax.ShapeDtypeStruct((slots, LANES), BF16),
        in_specs=[pl.BlockSpec(memory_space=pltpu.SMEM)] + vmem(5),
        out_specs=vmem(1)[0],
        scratch_shapes=[
            pltpu.VMEM((nrows, LANES), F32),
            pltpu.VMEM((slots + 8, LANES), F32),
            pltpu.VMEM((slots + 8, LANES), F32),
            pltpu.VMEM((nrows // LANES, LANES), I32),
            pltpu.SMEM((nrows // LANES, LANES), I32),
            pltpu.SemaphoreType.DMA,
        ],
        compiler_params=params(),
        name="dispatch",
    )(
        row_counts,
        radiances,
        owner_id.T,
        cell_index.T,
        valid_count.reshape(1, nrows),
        jacobian.T,
    )
    sent, background, turned = lax.optimization_barrier((sent, background, vertical.T))
    got = lax.all_to_all(
        sent.reshape(ndev, capacity, LANES), ("lon", "lat"), split_axis=0, concat_axis=0, tiled=True
    ).reshape(slots, LANES)
    ordered, mixer = pl.pallas_call(
        lambda *refs: prepare_kernel(lat_dev, *refs),
        out_shape=(
            jax.ShapeDtypeStruct((ncells, LANES), F32),
            jax.ShapeDtypeStruct((2 * LANES, 2 * LANES), BF16),
        ),
        in_specs=vmem(2),
        out_specs=tuple(vmem(2)),
        compiler_params=params(),
        cost_estimate=pl.CostEstimate(flops=0, bytes_accessed=12_000_000, transcendentals=0),
        name="prepare",
    )(background.reshape(ncells, levels), turned)
    acc = pltpu.VMEM((ncells + 8, LANES), F32)
    field = pl.pallas_call(
        lambda *refs: spread_kernel(capacity, lon_dev, lat_dev, levels, *refs),
        out_shape=jax.ShapeDtypeStruct(coded, I16),
        in_specs=[vmem(1)[0], pl.BlockSpec(memory_space=pl.ANY), vmem(1)[0]],
        out_specs=vmem(1)[0],
        scratch_shapes=[
            pltpu.VMEM((slots, LANES), F32),
            acc,
            acc,
            acc,
            acc,
            pltpu.VMEM((8, slots), I32),
            pltpu.SMEM((8, slots), I32),
            pltpu.SemaphoreType.DMA((2,)),
        ],
        compiler_params=params(),
        name="spread",
    )(got, ordered, mixer)

    half = n_lon * lon_dev // 2
    turned_kernel = jnp.roll(lon_kernel[::-1], 1)
    plus = turned_kernel[:half] + turned_kernel[half:]
    minus = turned_kernel[half:] - turned_kernel[:half]
    first = lon_kernel[:half] - lon_kernel[half:]
    minus = jnp.roll(first[::-1], 1)
    square = jax.ShapeDtypeStruct((half, half), BF16)
    toeplitz = pl.pallas_call(
        toeplitz_kernel,
        out_shape=(square,) * 4,
        in_specs=vmem(1),
        out_specs=tuple(vmem(4)),
        compiler_params=params(),
        name="toeplitz",
    )(jnp.stack([plus, minus]))

    columns = lax.all_to_all(field, "lon", split_axis=0, concat_axis=0, tiled=True)
    part = pltpu.VMEM((half, width), BF16)
    wide = pltpu.VMEM((half, width), F32)
    result = pl.pallas_call(
        conv_kernel,
        out_shape=jax.ShapeDtypeStruct(coded, I16),
        in_specs=vmem(1) + [pl.BlockSpec(memory_space=pl.ANY)] * 4,
        out_specs=vmem(1)[0],
        scratch_shapes=[pltpu.VMEM((half, half), BF16)] * 4
        + [part] * 4
        + [wide] * 2
        + [pltpu.SemaphoreType.DMA((4,))],
        compiler_params=params(),
        name="convolve",
    )(columns, *toeplitz)
    back = lax.all_to_all(result, "lon", split_axis=0, concat_axis=0, tiled=True)
    return pl.pallas_call(
        unpack_kernel,
        grid=(n_lon // 2,),
        out_shape=jax.ShapeDtypeStruct((lon_dev, lat_dev, levels), F32),
        in_specs=[pl.BlockSpec((2,) + coded[1:], lambda g: (g, 0, 0))],
        out_specs=pl.BlockSpec((lon_dev, 8, levels), lambda g: (0, g, 0)),
        compiler_params=params(),
        name="unpack",
    )(back)


def solution(mesh):
    return jax.shard_map(
        per_device,
        mesh=mesh,
        in_specs=(
            P(("lon", "lat"), None),
            P(("lon", "lat"), None),
            P(("lon", "lat"), None),
            P(("lon", "lat")),
            P(("lon", "lat")),
            P(),
            P("lon", "lat", None),
            P(),
            P(),
        ),
        out_specs=P("lon", "lat", None),
        check_vma=False,
    )
```

```python
import jax
import jax.numpy as jnp
from jax import lax
from jax.experimental import pallas as pl
from jax.experimental.pallas import tpu as pltpu
from jax.sharding import PartitionSpec as P

F32 = jnp.float32
BF16 = jnp.bfloat16
I32 = jnp.int32
I16 = jnp.int16
LANES = 128
TOP = 32700.0
LOWEST = -110.0
CODE_ROWS = 8


def vmem(n):
    return [pl.BlockSpec(memory_space=pltpu.VMEM)] * n


def params():
    return pltpu.CompilerParams(vmem_limit_bytes=56 * 1024 * 1024)


def quantise(tiles, out_ref, place):
    rows = tiles[0].shape[0]
    for k, tile in enumerate(tiles):
        top = jnp.max(jnp.abs(tile), axis=0, keepdims=True)
        power = jnp.maximum(jnp.ceil(jnp.log2(top)), LOWEST)
        factor = jnp.exp2(-power) * TOP
        digits = jnp.round(tile * factor)
        codes = jnp.broadcast_to(power, (CODE_ROWS, LANES))
        whole = jnp.concatenate([digits, codes], axis=0).astype(I32)
        out_ref[place, :, k * LANES : (k + 1) * LANES] = whole.astype(I16)


def dequantise(in_ref, place):
    whole = in_ref[place].astype(I32).astype(F32)
    rows = whole.shape[0] - CODE_ROWS
    factor = jnp.exp2(whole[rows : rows + 1]) * (1.0 / TOP)
    return whole[:rows] * factor


def split(x):
    high = x.astype(BF16)
    low = (x - high.astype(F32)).astype(BF16)
    return high, low


def dispatch_kernel(
    capacity,
    live_ref,
    rad_ref,
    owner_ref,
    cell_ref,
    count_ref,
    jac_ref,
    out_ref,
    pay_ref,
    even_ref,
    odd_ref,
    slot_v,
    slot_s,
    sem,
):
    nrows = rad_ref.shape[0]
    levels = jac_ref.shape[0]
    slots = out_ref.shape[0]
    ndev = slots // capacity
    foot = cell_ref.shape[0]
    n_live = live_ref[0]
    block = 256
    owner_ids = lax.broadcasted_iota(I32, (ndev, block), 0)
    earlier = (
        lax.broadcasted_iota(I32, (block, block), 0) < lax.broadcasted_iota(I32, (block, block), 1)
    ).astype(F32).astype(BF16)
    carry = jnp.zeros((ndev, 1), F32)
    for b in range(nrows // block):
        cols = slice(b * block, (b + 1) * block)
        position = lax.broadcasted_iota(I32, (1, block), 1) + b * block
        live = position < n_live
        owner = owner_ref[:, cols]
        hit = ((owner_ids == owner) & live).astype(F32)
        before = jnp.dot(hit.astype(BF16), earlier, preferred_element_type=F32) + carry
        rank = jnp.sum(hit * before, axis=0, keepdims=True).astype(I32)
        carry = carry + jnp.sum(hit, axis=1, keepdims=True)
        slot = jnp.where(live, owner * capacity + rank, slots)
        for i in range(block // LANES):
            row = b * (block // LANES) + i
            slot_v[:, row * LANES : (row + 1) * LANES] = slot[:, i * LANES : (i + 1) * LANES]
    copy = pltpu.make_async_copy(slot_v.at[0], slot_s, sem)
    copy.start()
    for b in range(nrows // block):
        cols = slice(b * block, (b + 1) * block)
        profile = lax.dot_general(
            jac_ref[...], rad_ref[cols, :], (((1,), (1,)), ((), ())), preferred_element_type=F32
        )
        count = count_ref[:, cols]
        share = (profile * (1.0 / count.astype(F32))).astype(BF16).astype(F32)
        cell = cell_ref[:, cols]
        used = lax.broadcasted_iota(I32, (foot, block), 0) < count
        lon = jnp.where(used, cell // 64, 0).astype(F32)
        lat = jnp.where(used, cell % 64, 64).astype(F32)
        rest = jnp.where(
            lax.broadcasted_iota(I32, (LANES - levels - 2 * foot, block), 0) == 0, 1.0, 0.0
        )
        payload = jnp.concatenate([share, jnp.concatenate([lon, lat], axis=0), rest], axis=0)
        pay_ref[cols, :] = payload.T
    even_ref[...] = jnp.zeros_like(even_ref)
    odd_ref[...] = jnp.zeros_like(odd_ref)
    copy.wait()
    unroll = 16

    def move(c, _):
        for u in range(unroll):
            slot = slot_s[c * unroll + u]
            to_ref = odd_ref if u % 2 else even_ref
            to_ref[pl.ds(slot, 1), :] = pay_ref[pl.ds(c * unroll + u, 1), :]
        return 0

    lax.fori_loop(0, (n_live + unroll - 1) // unroll, move, 0)
    out_ref[...] = (even_ref[:slots, :] + odd_ref[:slots, :]).astype(BF16)


def spread_kernel(
    capacity,
    lon_dev,
    lat_dev,
    levels,
    got_ref,
    back_ref,
    mix_ref,
    out_ref,
    share_ref,
    acc0,
    acc1,
    acc2,
    acc3,
    fields_v,
    meta_v,
    sems,
    *tables,
):
    slots = got_ref.shape[0]
    ndev = slots // capacity
    ncells = lon_dev * lat_dev
    foot = 4
    load = pltpu.make_async_copy(back_ref, acc0.at[pl.ds(0, ncells), :], sems.at[0])
    load.start()
    chunk = 8
    span = foot * chunk
    row_i = lax.broadcasted_iota(I32, (LANES, LANES), 0) - levels
    lane_i = lax.broadcasted_iota(I32, (LANES, LANES), 1)
    pick = (row_i >= 0) & (row_i <= 2 * foot) & (row_i == lane_i // chunk)
    pick = jnp.where(pick, 1.0, 0.0).astype(BF16)
    block = 256
    own = lax.broadcasted_iota(I32, (block, LANES), 0) % chunk
    own = own == lax.broadcasted_iota(I32, (block, LANES), 1) % chunk
    chunk_i = lax.broadcasted_iota(I32, (block // chunk, block), 0)
    gather = chunk_i == lax.broadcasted_iota(I32, (block // chunk, block), 1) // chunk
    gather = jnp.where(gather, 1.0, 0.0).astype(BF16)
    is_cell = lax.broadcasted_iota(I32, (block // chunk, LANES), 1) < span
    for b in range(slots // block):
        rows = slice(b * block, (b + 1) * block)
        part = got_ref[rows, :]
        fields = jnp.dot(part, pick, preferred_element_type=F32)
        fields = jnp.where(own, fields, 0.0).astype(BF16)
        table = jnp.dot(gather, fields, preferred_element_type=F32)
        turned = pltpu.roll(table, LANES - span, 1)
        table = jnp.where(is_cell, table + turned * float(lon_dev), table)
        at = b * (block // chunk)
        fields_v[at : at + block // chunk, :] = table
        share_ref[rows, :] = part.astype(F32)
    lanes = list(range(span)) + [2 * span]
    for i in range(slots // chunk // LANES):
        cols = slice(i * LANES, (i + 1) * LANES)
        turned = fields_v[cols, :].T.astype(I32)
        for k, lane in enumerate(lanes):
            meta_v[k, :, cols] = turned[lane : lane + 1, :]
    copies = [pltpu.make_async_copy(meta_v.at[k, 0], t, sems.at[k + 1]) for k, t in enumerate(tables)]
    for copy in copies:
        copy.start()
    accs = (acc0, acc1, acc2, acc3)
    for acc in accs[1:]:
        acc[...] = jnp.zeros_like(acc)
    load.wait()
    for copy in copies:
        copy.wait()
    per_source = capacity // chunk

    def one_source(s, _):
        base = s * per_source
        n_chunks = tables[span][base]
        for c in range(1, per_source):
            n_chunks = n_chunks + tables[span][base + c]

        def one_chunk(c, _):
            first = pl.multiple_of(c * chunk, chunk)
            for u in range(chunk):
                row = share_ref[pl.ds(first + u, 1), :]
                for f in range(foot):
                    cell = tables[f * chunk + u][c]
                    accs[f][pl.ds(cell, 1), :] = accs[f][pl.ds(cell, 1), :] + row
            return 0

        lax.fori_loop(base, base + n_chunks, one_chunk, 0)
        return 0

    lax.fori_loop(0, ndev, one_source, 0)
    lane = lax.broadcasted_iota(I32, (lon_dev, LANES), 1)

    def one_group(t, _):
        rows = pl.ds(pl.multiple_of(t * 4 * lon_dev, 4 * lon_dev), 4 * lon_dev)
        total = (acc0[rows, :] + acc1[rows, :]) + (acc2[rows, :] + acc3[rows, :])
        high, low = split(total)
        both = jnp.dot(
            jnp.concatenate([high, low], axis=1), mix_ref[...], preferred_element_type=F32
        )
        mixed = both[:, :LANES] + both[:, LANES:]
        a = [mixed[j * lon_dev : (j + 1) * lon_dev, :] for j in range(4)]
        r1 = pltpu.roll(a[1], 96, 1)
        r2 = pltpu.roll(a[2], 64, 1)
        r3 = pltpu.roll(a[3], 32, 1)
        tiles = [
            jnp.where(lane < 96, a[0], r1),
            jnp.where(lane < 64, r1, r2),
            jnp.where(lane < 32, r2, r3),
        ]
        quantise(tiles, out_ref, t)
        return 0

    lax.fori_loop(0, ncells // (4 * lon_dev), one_group, 0, unroll=4)


def prepare_kernel(lat_dev, back_ref, vert_ref, out_ref, mix_ref):
    ncells, levels = back_ref.shape
    lon_dev = ncells // lat_dev
    v_high, v_low = split(vert_ref[...].T)
    mix_ref[...] = jnp.zeros_like(mix_ref)
    mix_ref[:levels, :levels] = v_high
    mix_ref[:levels, LANES : LANES + levels] = v_low
    mix_ref[LANES : LANES + levels, :levels] = v_high
    out_ref[...] = jnp.zeros_like(out_ref)
    for lat in range(lat_dev):
        out_ref[lat * lon_dev : (lat + 1) * lon_dev, :levels] = back_ref[
            pl.ds(lat, lon_dev, stride=lat_dev), :
        ]


def toeplitz_kernel(kern_ref, ph_ref, pl_ref, mh_ref, ml_ref):
    n = kern_ref.shape[1]
    block = 256
    for high_ref, low_ref, row, sign in ((ph_ref, pl_ref, 0, False), (mh_ref, ml_ref, 1, True)):
        base = jnp.broadcast_to(kern_ref[row : row + 1, :], (block, n))
        strip = pltpu.roll(base, 0, 1, stride=1, stride_axis=0)
        for i in range(n // block):
            if i:
                strip = jnp.concatenate([strip[:, n - block :], strip[:, : n - block]], axis=1)
            piece = strip
            if sign:
                row_i = lax.broadcasted_iota(I32, (block, n), 0) + i * block
                piece = jnp.where(lax.broadcasted_iota(I32, (block, n), 1) > row_i, -strip, strip)
            high, low = split(piece)
            high_ref[i * block : (i + 1) * block, :] = high
            low_ref[i * block : (i + 1) * block, :] = low


def conv_kernel(got_ref, *refs):
    hbm, out_ref, held, (xph, xpl, xmh, xml, yp, ym, sems) = refs[:4], refs[4], refs[5:9], refs[9:]
    loads = [pltpu.make_async_copy(a, b, sems.at[i]) for i, (a, b) in enumerate(zip(hbm, held))]
    for load in loads:
        load.start()
    ph_ref, pl_ref, mh_ref, ml_ref = held
    n_lon = got_ref.shape[0]
    rows = got_ref.shape[1] - CODE_ROWS
    half = n_lon // 2
    for s in range(half):
        a = dequantise(got_ref, s)
        b = dequantise(got_ref, s + half)
        at = slice(s * rows, (s + 1) * rows)
        xph[at, :], xpl[at, :] = split(a + b)
        xmh[at, :], xml[at, :] = split(a - b)
    for load in loads:
        load.wait()
    for th, tl, xh, xl, y in ((ph_ref, pl_ref, xph, xpl, yp), (mh_ref, ml_ref, xmh, xml, ym)):
        y[...] = (
            jnp.dot(th[...], xh[...], preferred_element_type=F32)
            + jnp.dot(tl[...], xh[...], preferred_element_type=F32)
            + jnp.dot(th[...], xl[...], preferred_element_type=F32)
        )
    width = got_ref.shape[2]
    for s in range(half):
        at = slice(s * rows, (s + 1) * rows)
        plus, minus = yp[at, :], ym[at, :]
        for place, y in ((s, 0.5 * (plus + minus)), (s + half, 0.5 * (plus - minus))):
            quantise([y[:, k : k + LANES] for k in range(0, width, LANES)], out_ref, place)


def unpack_kernel(got_ref, out_ref, held_ref):
    lon_dev, lats, levels = out_ref.shape
    lane = lax.broadcasted_iota(I32, (lon_dev, LANES), 1)
    for t in range(got_ref.shape[0]):
        x = dequantise(got_ref, t)
        o = [x[:, k * LANES : (k + 1) * LANES] for k in range(3)]
        a = [
            o[0],
            pltpu.roll(jnp.where(lane >= 96, o[0], o[1]), 32, 1),
            pltpu.roll(jnp.where(lane >= 64, o[1], o[2]), 64, 1),
            pltpu.roll(o[2], 96, 1),
        ]
        for j in range(4):
            at = (t * 4 + j) * lon_dev
            held_ref[at : at + lon_dev, :] = a[j]
    for i in range(lon_dev):
        out_ref[i] = held_ref[pl.ds(i, lats, stride=lon_dev), :][:, :levels]


def per_device(
    radiances,
    owner_id,
    cell_index,
    valid_count,
    row_counts,
    jacobian,
    background,
    vertical,
    lon_kernel,
):
    n_lon = lax.axis_size("lon")
    ndev = n_lon * lax.axis_size("lat")
    nrows = radiances.shape[0]
    lon_dev, lat_dev, levels = background.shape
    capacity = 5 * nrows // (2 * ndev)
    slots = ndev * capacity
    ncells = lon_dev * lat_dev
    width = ncells // n_lon // lon_dev * levels
    coded = (n_lon, lon_dev + CODE_ROWS, width)

    sent = pl.pallas_call(
        lambda *refs: dispatch_kernel(capacity, *refs),
        out_shape=jax.ShapeDtypeStruct((slots, LANES), BF16),
        in_specs=[pl.BlockSpec(memory_space=pltpu.SMEM)] + vmem(5),
        out_specs=vmem(1)[0],
        scratch_shapes=[
            pltpu.VMEM((nrows, LANES), F32),
            pltpu.VMEM((slots + 8, LANES), F32),
            pltpu.VMEM((slots + 8, LANES), F32),
            pltpu.VMEM((1, nrows), I32),
            pltpu.SMEM((nrows,), I32),
            pltpu.SemaphoreType.DMA,
        ],
        compiler_params=params(),
        name="dispatch",
    )(
        row_counts,
        radiances,
        owner_id.T,
        cell_index.T,
        valid_count.reshape(1, nrows),
        jacobian.T,
    )
    sent, background, vertical = lax.optimization_barrier((sent, background, vertical))
    got = lax.all_to_all(
        sent.reshape(ndev, capacity, LANES), ("lon", "lat"), split_axis=0, concat_axis=0, tiled=True
    ).reshape(slots, LANES)
    ordered, mixer = pl.pallas_call(
        lambda *refs: prepare_kernel(lat_dev, *refs),
        out_shape=(
            jax.ShapeDtypeStruct((ncells, LANES), F32),
            jax.ShapeDtypeStruct((2 * LANES, 2 * LANES), BF16),
        ),
        in_specs=vmem(2),
        out_specs=tuple(vmem(2)),
        compiler_params=params(),
        cost_estimate=pl.CostEstimate(flops=0, bytes_accessed=12_000_000, transcendentals=0),
        name="prepare",
    )(background.reshape(ncells, levels), vertical)
    acc = pltpu.VMEM((ncells + 8, LANES), F32)
    field = pl.pallas_call(
        lambda *refs: spread_kernel(capacity, lon_dev, lat_dev, levels, *refs),
        out_shape=jax.ShapeDtypeStruct(coded, I16),
        in_specs=[vmem(1)[0], pl.BlockSpec(memory_space=pl.ANY), vmem(1)[0]],
        out_specs=vmem(1)[0],
        scratch_shapes=[
            pltpu.VMEM((slots, LANES), F32),
            acc,
            acc,
            acc,
            acc,
            pltpu.VMEM((slots // 8, LANES), F32),
            pltpu.VMEM((33, 1, slots // 8), I32),
            pltpu.SemaphoreType.DMA((34,)),
        ]
        + [pltpu.SMEM((slots // 8,), I32)] * 33,
        compiler_params=params(),
        name="spread",
    )(got, ordered, mixer)

    half = n_lon * lon_dev // 2
    turned_kernel = jnp.roll(lon_kernel[::-1], 1)
    plus = turned_kernel[:half] + turned_kernel[half:]
    minus = turned_kernel[half:] - turned_kernel[:half]
    first = lon_kernel[:half] - lon_kernel[half:]
    minus = jnp.roll(first[::-1], 1)
    square = jax.ShapeDtypeStruct((half, half), BF16)
    toeplitz = pl.pallas_call(
        toeplitz_kernel,
        out_shape=(square,) * 4,
        in_specs=vmem(1),
        out_specs=tuple(vmem(4)),
        compiler_params=params(),
        name="toeplitz",
    )(jnp.stack([plus, minus]))

    columns = lax.all_to_all(field, "lon", split_axis=0, concat_axis=0, tiled=True)
    part = pltpu.VMEM((half, width), BF16)
    wide = pltpu.VMEM((half, width), F32)
    result = pl.pallas_call(
        conv_kernel,
        out_shape=jax.ShapeDtypeStruct(coded, I16),
        in_specs=vmem(1) + [pl.BlockSpec(memory_space=pl.ANY)] * 4,
        out_specs=vmem(1)[0],
        scratch_shapes=[pltpu.VMEM((half, half), BF16)] * 4
        + [part] * 4
        + [wide] * 2
        + [pltpu.SemaphoreType.DMA((4,))],
        compiler_params=params(),
        name="convolve",
    )(columns, *toeplitz)
    back = lax.all_to_all(result, "lon", split_axis=0, concat_axis=0, tiled=True)
    return pl.pallas_call(
        unpack_kernel,
        grid=(n_lon // 2,),
        out_shape=jax.ShapeDtypeStruct((lon_dev, lat_dev, levels), F32),
        in_specs=[pl.BlockSpec((2,) + coded[1:], lambda g: (g, 0, 0))],
        out_specs=pl.BlockSpec((lon_dev, 8, levels), lambda g: (0, g, 0)),
        scratch_shapes=[pltpu.VMEM((8 * lon_dev, LANES), F32)],
        compiler_params=params(),
        name="unpack",
    )(back)


def solution(mesh):
    return jax.shard_map(
        per_device,
        mesh=mesh,
        in_specs=(
            P(("lon", "lat"), None),
            P(("lon", "lat"), None),
            P(("lon", "lat"), None),
            P(("lon", "lat")),
            P(("lon", "lat")),
            P(),
            P("lon", "lat", None),
            P(),
            P(),
        ),
        out_specs=P("lon", "lat", None),
        check_vma=False,
    )
```

```python
import jax
import jax.numpy as jnp
from jax import lax
from jax.experimental import pallas as pl
from jax.experimental.pallas import tpu as pltpu
from jax.sharding import PartitionSpec as P

F32 = jnp.float32
BF16 = jnp.bfloat16
I32 = jnp.int32
I16 = jnp.int16
LANES = 128
N_ACC = 8
TOP = 32700.0
LOWEST = -110.0
CODE_ROWS = 8


def vmem(n):
    return [pl.BlockSpec(memory_space=pltpu.VMEM)] * n


def params():
    return pltpu.CompilerParams(vmem_limit_bytes=56 * 1024 * 1024)


def quantise(tiles, out_ref, place):
    rows = tiles[0].shape[0]
    for k, tile in enumerate(tiles):
        top = jnp.max(jnp.abs(tile), axis=0, keepdims=True)
        power = jnp.maximum(jnp.ceil(jnp.log2(top)), LOWEST)
        factor = jnp.exp2(-power) * TOP
        digits = jnp.round(tile * factor)
        codes = jnp.broadcast_to(power, (CODE_ROWS, LANES))
        whole = jnp.concatenate([digits, codes], axis=0).astype(I32)
        out_ref[place, :, k * LANES : (k + 1) * LANES] = whole.astype(I16)


def dequantise(in_ref, place):
    whole = in_ref[place].astype(I32).astype(F32)
    rows = whole.shape[0] - CODE_ROWS
    factor = jnp.exp2(whole[rows : rows + 1]) * (1.0 / TOP)
    return whole[:rows] * factor


def split(x):
    high = x.astype(BF16)
    low = (x - high.astype(F32)).astype(BF16)
    return high, low


def dispatch_kernel(
    capacity,
    live_ref,
    rad_ref,
    owner_ref,
    cell_ref,
    count_ref,
    jac_ref,
    out_ref,
    pay_ref,
    even_ref,
    odd_ref,
    slot_v,
    slot_s,
    sem,
):
    nrows = rad_ref.shape[0]
    levels = jac_ref.shape[0]
    slots = out_ref.shape[0]
    ndev = slots // capacity
    foot = cell_ref.shape[0]
    n_live = live_ref[0]
    block = 256
    owner_ids = lax.broadcasted_iota(I32, (ndev, block), 0)
    earlier = (
        lax.broadcasted_iota(I32, (block, block), 0) < lax.broadcasted_iota(I32, (block, block), 1)
    ).astype(F32).astype(BF16)
    carry = jnp.zeros((ndev, 1), F32)
    for b in range(nrows // block):
        cols = slice(b * block, (b + 1) * block)
        position = lax.broadcasted_iota(I32, (1, block), 1) + b * block
        live = position < n_live
        owner = owner_ref[:, cols]
        hit = ((owner_ids == owner) & live).astype(F32)
        before = jnp.dot(hit.astype(BF16), earlier, preferred_element_type=F32) + carry
        rank = jnp.sum(hit * before, axis=0, keepdims=True).astype(I32)
        carry = carry + jnp.sum(hit, axis=1, keepdims=True)
        slot = jnp.where(live, owner * capacity + rank, slots)
        for i in range(block // LANES):
            row = b * (block // LANES) + i
            slot_v[:, row * LANES : (row + 1) * LANES] = slot[:, i * LANES : (i + 1) * LANES]
    copy = pltpu.make_async_copy(slot_v.at[0], slot_s, sem)
    copy.start()
    for b in range(nrows // block):
        cols = slice(b * block, (b + 1) * block)
        profile = lax.dot_general(
            jac_ref[...], rad_ref[cols, :], (((1,), (1,)), ((), ())), preferred_element_type=F32
        )
        count = count_ref[:, cols]
        share = (profile * (1.0 / count.astype(F32))).astype(BF16).astype(F32)
        cell = cell_ref[:, cols]
        used = lax.broadcasted_iota(I32, (foot, block), 0) < count
        lon = jnp.where(used, cell // 64, 0).astype(F32)
        lat = jnp.where(used, cell % 64, 64).astype(F32)
        rest = jnp.where(
            lax.broadcasted_iota(I32, (LANES - levels - 2 * foot, block), 0) == 0, 1.0, 0.0
        )
        payload = jnp.concatenate([share, jnp.concatenate([lon, lat], axis=0), rest], axis=0)
        pay_ref[cols, :] = payload.T
    even_ref[...] = jnp.zeros_like(even_ref)
    odd_ref[...] = jnp.zeros_like(odd_ref)
    copy.wait()
    unroll = 16

    def move(c, _):
        for u in range(unroll):
            slot = slot_s[c * unroll + u]
            to_ref = odd_ref if u % 2 else even_ref
            to_ref[pl.ds(slot, 1), :] = pay_ref[pl.ds(c * unroll + u, 1), :]
        return 0

    lax.fori_loop(0, (n_live + unroll - 1) // unroll, move, 0)
    out_ref[...] = (even_ref[:slots, :] + odd_ref[:slots, :]).astype(BF16)


def spread_kernel(
    capacity,
    lon_dev,
    lat_dev,
    levels,
    got_ref,
    back_ref,
    mix_ref,
    out_ref,
    share_ref,
    fields_v,
    meta_v,
    sems,
    *held,
):
    accs, tables = held[:N_ACC], held[N_ACC:]
    slots = got_ref.shape[0]
    ndev = slots // capacity
    ncells = lon_dev * lat_dev
    foot = 4
    load = pltpu.make_async_copy(back_ref, accs[0].at[pl.ds(0, ncells), :], sems.at[0])
    load.start()
    chunk = 8
    span = foot * chunk
    row_i = lax.broadcasted_iota(I32, (LANES, LANES), 0) - levels
    lane_i = lax.broadcasted_iota(I32, (LANES, LANES), 1)
    pick = (row_i >= 0) & (row_i <= 2 * foot) & (row_i == lane_i // chunk)
    pick = jnp.where(pick, 1.0, 0.0).astype(BF16)
    block = 256
    own = lax.broadcasted_iota(I32, (block, LANES), 0) % chunk
    own = own == lax.broadcasted_iota(I32, (block, LANES), 1) % chunk
    chunk_i = lax.broadcasted_iota(I32, (block // chunk, block), 0)
    gather = chunk_i == lax.broadcasted_iota(I32, (block // chunk, block), 1) // chunk
    gather = jnp.where(gather, 1.0, 0.0).astype(BF16)
    is_cell = lax.broadcasted_iota(I32, (block // chunk, LANES), 1) < span
    for b in range(slots // block):
        rows = slice(b * block, (b + 1) * block)
        part = got_ref[rows, :]
        fields = jnp.dot(part, pick, preferred_element_type=F32)
        fields = jnp.where(own, fields, 0.0).astype(BF16)
        table = jnp.dot(gather, fields, preferred_element_type=F32)
        turned = pltpu.roll(table, LANES - span, 1)
        table = jnp.where(is_cell, table + turned * float(lon_dev), table)
        at = b * (block // chunk)
        fields_v[at : at + block // chunk, :] = table
    lanes = list(range(span)) + [2 * span]
    for i in range(slots // chunk // LANES):
        cols = slice(i * LANES, (i + 1) * LANES)
        turned = fields_v[cols, :].T.astype(I32)
        for k, lane in enumerate(lanes):
            meta_v[k, :, cols] = turned[lane : lane + 1, :]
    copies = [pltpu.make_async_copy(meta_v.at[k, 0], t, sems.at[k + 1]) for k, t in enumerate(tables)]
    for copy in copies:
        copy.start()
    share_ref[...] = got_ref[...].astype(F32)
    for acc in accs[1:]:
        acc[...] = jnp.zeros_like(acc)
    load.wait()
    for copy in copies:
        copy.wait()
    per_source = capacity // chunk

    def one_source(s, _):
        base = s * per_source
        n_chunks = tables[span][base]
        for c in range(1, per_source):
            n_chunks = n_chunks + tables[span][base + c]

        def one_chunk(c, _):
            first = pl.multiple_of(c * chunk, chunk)
            for u in range(chunk):
                row = share_ref[pl.ds(first + u, 1), :]
                for f in range(foot):
                    cell = tables[f * chunk + u][c]
                    acc = accs[(u * foot + f) % N_ACC]
                    acc[pl.ds(cell, 1), :] = acc[pl.ds(cell, 1), :] + row
            return 0

        lax.fori_loop(base, base + n_chunks, one_chunk, 0)
        return 0

    lax.fori_loop(0, ndev, one_source, 0)
    lane = lax.broadcasted_iota(I32, (lon_dev, LANES), 1)

    def one_group(t, _):
        rows = pl.ds(pl.multiple_of(t * 4 * lon_dev, 4 * lon_dev), 4 * lon_dev)
        sums = [acc[rows, :] for acc in accs]
        while len(sums) > 1:
            sums = [a + b for a, b in zip(sums[::2], sums[1::2])]
        total = sums[0]
        high, low = split(total)
        both = jnp.dot(
            jnp.concatenate([high, low], axis=1), mix_ref[...], preferred_element_type=F32
        )
        mixed = both[:, :LANES] + both[:, LANES:]
        a = [mixed[j * lon_dev : (j + 1) * lon_dev, :] for j in range(4)]
        r1 = pltpu.roll(a[1], 96, 1)
        r2 = pltpu.roll(a[2], 64, 1)
        r3 = pltpu.roll(a[3], 32, 1)
        tiles = [
            jnp.where(lane < 96, a[0], r1),
            jnp.where(lane < 64, r1, r2),
            jnp.where(lane < 32, r2, r3),
        ]
        quantise(tiles, out_ref, t)
        return 0

    lax.fori_loop(0, ncells // (4 * lon_dev), one_group, 0, unroll=4)


def prepare_kernel(lat_dev, back_ref, vert_ref, out_ref, mix_ref):
    ncells, levels = back_ref.shape
    lon_dev = ncells // lat_dev
    v_high, v_low = split(vert_ref[...].T)
    mix_ref[...] = jnp.zeros_like(mix_ref)
    mix_ref[:levels, :levels] = v_high
    mix_ref[:levels, LANES : LANES + levels] = v_low
    mix_ref[LANES : LANES + levels, :levels] = v_high
    out_ref[...] = jnp.zeros_like(out_ref)
    for lat in range(lat_dev):
        out_ref[lat * lon_dev : (lat + 1) * lon_dev, :levels] = back_ref[
            pl.ds(lat, lon_dev, stride=lat_dev), :
        ]


def toeplitz_kernel(kern_ref, ph_ref, pl_ref, mh_ref, ml_ref):
    n = kern_ref.shape[1]
    block = 256
    for high_ref, low_ref, row, sign in ((ph_ref, pl_ref, 0, False), (mh_ref, ml_ref, 1, True)):
        base = jnp.broadcast_to(kern_ref[row : row + 1, :], (block, n))
        strip = pltpu.roll(base, 0, 1, stride=1, stride_axis=0)
        for i in range(n // block):
            if i:
                strip = jnp.concatenate([strip[:, n - block :], strip[:, : n - block]], axis=1)
            piece = strip
            if sign:
                row_i = lax.broadcasted_iota(I32, (block, n), 0) + i * block
                piece = jnp.where(lax.broadcasted_iota(I32, (block, n), 1) > row_i, -strip, strip)
            high, low = split(piece)
            high_ref[i * block : (i + 1) * block, :] = high
            low_ref[i * block : (i + 1) * block, :] = low


def conv_kernel(got_ref, *refs):
    hbm, out_ref, held, (xph, xpl, xmh, xml, yp, ym, sems) = refs[:4], refs[4], refs[5:9], refs[9:]
    loads = [pltpu.make_async_copy(a, b, sems.at[i]) for i, (a, b) in enumerate(zip(hbm, held))]
    for load in loads:
        load.start()
    ph_ref, pl_ref, mh_ref, ml_ref = held
    n_lon = got_ref.shape[0]
    rows = got_ref.shape[1] - CODE_ROWS
    half = n_lon // 2
    for s in range(half):
        a = dequantise(got_ref, s)
        b = dequantise(got_ref, s + half)
        at = slice(s * rows, (s + 1) * rows)
        xph[at, :], xpl[at, :] = split(a + b)
        xmh[at, :], xml[at, :] = split(a - b)
    for load in loads:
        load.wait()
    for th, tl, xh, xl, y in ((ph_ref, pl_ref, xph, xpl, yp), (mh_ref, ml_ref, xmh, xml, ym)):
        y[...] = (
            jnp.dot(th[...], xh[...], preferred_element_type=F32)
            + jnp.dot(tl[...], xh[...], preferred_element_type=F32)
            + jnp.dot(th[...], xl[...], preferred_element_type=F32)
        )
    width = got_ref.shape[2]
    for s in range(half):
        at = slice(s * rows, (s + 1) * rows)
        plus, minus = yp[at, :], ym[at, :]
        for place, y in ((s, 0.5 * (plus + minus)), (s + half, 0.5 * (plus - minus))):
            quantise([y[:, k : k + LANES] for k in range(0, width, LANES)], out_ref, place)


def unpack_kernel(got_ref, out_ref, held_ref):
    lon_dev, lats, levels = out_ref.shape
    lane = lax.broadcasted_iota(I32, (lon_dev, LANES), 1)
    for t in range(got_ref.shape[0]):
        x = dequantise(got_ref, t)
        o = [x[:, k * LANES : (k + 1) * LANES] for k in range(3)]
        a = [
            o[0],
            pltpu.roll(jnp.where(lane >= 96, o[0], o[1]), 32, 1),
            pltpu.roll(jnp.where(lane >= 64, o[1], o[2]), 64, 1),
            pltpu.roll(o[2], 96, 1),
        ]
        for j in range(4):
            at = (t * 4 + j) * lon_dev
            held_ref[at : at + lon_dev, :] = a[j]
    for i in range(lon_dev):
        for g in range(0, lats, 8):
            picked = held_ref[pl.ds(g * lon_dev + i, 8, stride=lon_dev), :]
            out_ref[i, g : g + 8, :] = picked[:, :levels]


def call_spread(got, ordered, mixer, capacity, lon_dev, lat_dev, levels, coded):
    slots = got.shape[0]
    ncells = lon_dev * lat_dev
    acc = pltpu.VMEM((ncells + 8, LANES), F32)
    return pl.pallas_call(
        lambda *refs: spread_kernel(capacity, lon_dev, lat_dev, levels, *refs),
        out_shape=jax.ShapeDtypeStruct(coded, I16),
        in_specs=[vmem(1)[0], pl.BlockSpec(memory_space=pl.ANY), vmem(1)[0]],
        out_specs=vmem(1)[0],
        scratch_shapes=[
            pltpu.VMEM((slots, LANES), F32),
            pltpu.VMEM((slots // 8, LANES), F32),
            pltpu.VMEM((33, 1, slots // 8), I32),
            pltpu.SemaphoreType.DMA((34,)),
        ]
        + [acc] * N_ACC
        + [pltpu.SMEM((slots // 8,), I32)] * 33,
        compiler_params=params(),
        name="spread",
    )(got, ordered, mixer)


def call_convolve(columns, toeplitz, half, width, coded):
    part = pltpu.VMEM((half, width), BF16)
    wide = pltpu.VMEM((half, width), F32)
    return pl.pallas_call(
        conv_kernel,
        out_shape=jax.ShapeDtypeStruct(coded, I16),
        in_specs=vmem(1) + [pl.BlockSpec(memory_space=pl.ANY)] * 4,
        out_specs=vmem(1)[0],
        scratch_shapes=[pltpu.VMEM((half, half), BF16)] * 4
        + [part] * 4
        + [wide] * 2
        + [pltpu.SemaphoreType.DMA((4,))],
        compiler_params=params(),
        name="convolve",
    )(columns, *toeplitz)


def call_unpack(back, lon_dev, lat_dev, levels, coded):
    n_lon = coded[0]
    return pl.pallas_call(
        unpack_kernel,
        grid=(n_lon // 4,),
        out_shape=jax.ShapeDtypeStruct((lon_dev, lat_dev, levels), F32),
        in_specs=[pl.BlockSpec((4,) + coded[1:], lambda g: (g, 0, 0))],
        out_specs=pl.BlockSpec((lon_dev, 16, levels), lambda g: (0, g, 0)),
        scratch_shapes=[pltpu.VMEM((16 * lon_dev, LANES), F32)],
        compiler_params=params(),
        name="unpack",
    )(back)


def per_device(
    radiances,
    owner_id,
    cell_index,
    valid_count,
    row_counts,
    jacobian,
    background,
    vertical,
    lon_kernel,
):
    n_lon = lax.axis_size("lon")
    ndev = n_lon * lax.axis_size("lat")
    nrows = radiances.shape[0]
    lon_dev, lat_dev, levels = background.shape
    capacity = 5 * nrows // (2 * ndev)
    slots = ndev * capacity
    ncells = lon_dev * lat_dev
    width = ncells // n_lon // lon_dev * levels
    coded = (n_lon, lon_dev + CODE_ROWS, width)

    sent = pl.pallas_call(
        lambda *refs: dispatch_kernel(capacity, *refs),
        out_shape=jax.ShapeDtypeStruct((slots, LANES), BF16),
        in_specs=[pl.BlockSpec(memory_space=pltpu.SMEM)] + vmem(5),
        out_specs=vmem(1)[0],
        scratch_shapes=[
            pltpu.VMEM((nrows, LANES), F32),
            pltpu.VMEM((slots + 8, LANES), F32),
            pltpu.VMEM((slots + 8, LANES), F32),
            pltpu.VMEM((1, nrows), I32),
            pltpu.SMEM((nrows,), I32),
            pltpu.SemaphoreType.DMA,
        ],
        compiler_params=params(),
        name="dispatch",
    )(
        row_counts,
        radiances,
        owner_id.T,
        cell_index.T,
        valid_count.reshape(1, nrows),
        jacobian.T,
    )
    sent, background, vertical = lax.optimization_barrier((sent, background, vertical))
    got = lax.all_to_all(
        sent.reshape(ndev, capacity, LANES), ("lon", "lat"), split_axis=0, concat_axis=0, tiled=True
    ).reshape(slots, LANES)
    ordered, mixer = pl.pallas_call(
        lambda *refs: prepare_kernel(lat_dev, *refs),
        out_shape=(
            jax.ShapeDtypeStruct((ncells, LANES), F32),
            jax.ShapeDtypeStruct((2 * LANES, 2 * LANES), BF16),
        ),
        in_specs=vmem(2),
        out_specs=tuple(vmem(2)),
        compiler_params=params(),
        cost_estimate=pl.CostEstimate(flops=0, bytes_accessed=12_000_000, transcendentals=0),
        name="prepare",
    )(background.reshape(ncells, levels), vertical)
    field = call_spread(got, ordered, mixer, capacity, lon_dev, lat_dev, levels, coded)

    half = n_lon * lon_dev // 2
    turned_kernel = jnp.roll(lon_kernel[::-1], 1)
    plus = turned_kernel[:half] + turned_kernel[half:]
    minus = turned_kernel[half:] - turned_kernel[:half]
    first = lon_kernel[:half] - lon_kernel[half:]
    minus = jnp.roll(first[::-1], 1)
    square = jax.ShapeDtypeStruct((half, half), BF16)
    toeplitz = pl.pallas_call(
        toeplitz_kernel,
        out_shape=(square,) * 4,
        in_specs=vmem(1),
        out_specs=tuple(vmem(4)),
        compiler_params=params(),
        name="toeplitz",
    )(jnp.stack([plus, minus]))

    columns = lax.all_to_all(field, "lon", split_axis=0, concat_axis=0, tiled=True)
    result = call_convolve(columns, toeplitz, half, width, coded)
    back = lax.all_to_all(result, "lon", split_axis=0, concat_axis=0, tiled=True)
    return call_unpack(back, lon_dev, lat_dev, levels, coded)


def solution(mesh):
    return jax.shard_map(
        per_device,
        mesh=mesh,
        in_specs=(
            P(("lon", "lat"), None),
            P(("lon", "lat"), None),
            P(("lon", "lat"), None),
            P(("lon", "lat")),
            P(("lon", "lat")),
            P(),
            P("lon", "lat", None),
            P(),
            P(),
        ),
        out_specs=P("lon", "lat", None),
        check_vma=False,
    )
```

```python
import jax
import jax.numpy as jnp
from jax import lax
from jax.experimental import pallas as pl
from jax.experimental.pallas import tpu as pltpu
from jax.sharding import PartitionSpec as P

F32 = jnp.float32
BF16 = jnp.bfloat16
I32 = jnp.int32
I16 = jnp.int16
LANES = 128
N_ACC = 8
TOP = 32700.0
LOWEST = -110.0
CODE_ROWS = 8


def vmem(n):
    return [pl.BlockSpec(memory_space=pltpu.VMEM)] * n


def params(mib=56):
    return pltpu.CompilerParams(vmem_limit_bytes=mib * 1024 * 1024)


def quantise(tiles, out_ref, place):
    rows = tiles[0].shape[0]
    for k, tile in enumerate(tiles):
        top = jnp.max(jnp.abs(tile), axis=0, keepdims=True)
        power = jnp.maximum(jnp.ceil(jnp.log2(top)), LOWEST)
        factor = jnp.exp2(-power) * TOP
        digits = jnp.round(tile * factor)
        codes = jnp.broadcast_to(power, (CODE_ROWS, LANES))
        whole = jnp.concatenate([digits, codes], axis=0).astype(I32)
        out_ref[place, :, k * LANES : (k + 1) * LANES] = whole.astype(I16)


def dequantise(in_ref, place):
    whole = in_ref[place].astype(I32).astype(F32)
    rows = whole.shape[0] - CODE_ROWS
    factor = jnp.exp2(whole[rows : rows + 1]) * (1.0 / TOP)
    return whole[:rows] * factor


def split(x):
    high = x.astype(BF16)
    low = (x - high.astype(F32)).astype(BF16)
    return high, low


def dispatch_kernel(
    capacity,
    live_ref,
    rad_ref,
    owner_ref,
    cell_ref,
    count_ref,
    jac_ref,
    out_ref,
    pay_ref,
    even_ref,
    odd_ref,
    slot_v,
    slot_s,
    sem,
):
    nrows = rad_ref.shape[0]
    levels = jac_ref.shape[0]
    slots = out_ref.shape[0]
    ndev = slots // capacity
    foot = cell_ref.shape[0]
    n_live = live_ref[0]
    block = 256
    owner_ids = lax.broadcasted_iota(I32, (ndev, block), 0)
    earlier = (
        lax.broadcasted_iota(I32, (block, block), 0) < lax.broadcasted_iota(I32, (block, block), 1)
    ).astype(F32).astype(BF16)
    carry = jnp.zeros((ndev, 1), F32)
    for b in range(nrows // block):
        cols = slice(b * block, (b + 1) * block)
        position = lax.broadcasted_iota(I32, (1, block), 1) + b * block
        live = position < n_live
        owner = owner_ref[:, cols]
        hit = ((owner_ids == owner) & live).astype(F32)
        before = jnp.dot(hit.astype(BF16), earlier, preferred_element_type=F32) + carry
        rank = jnp.sum(hit * before, axis=0, keepdims=True).astype(I32)
        carry = carry + jnp.sum(hit, axis=1, keepdims=True)
        slot = jnp.where(live, owner * capacity + rank, slots)
        for i in range(block // LANES):
            row = b * (block // LANES) + i
            slot_v[:, row * LANES : (row + 1) * LANES] = slot[:, i * LANES : (i + 1) * LANES]
    copy = pltpu.make_async_copy(slot_v.at[0], slot_s, sem)
    copy.start()
    for b in range(nrows // block):
        cols = slice(b * block, (b + 1) * block)
        profile = lax.dot_general(
            jac_ref[...], rad_ref[cols, :], (((1,), (1,)), ((), ())), preferred_element_type=F32
        )
        count = count_ref[:, cols]
        share = (profile * (1.0 / count.astype(F32))).astype(BF16).astype(F32)
        cell = cell_ref[:, cols]
        used = lax.broadcasted_iota(I32, (foot, block), 0) < count
        lon = jnp.where(used, cell // 64, 0).astype(F32)
        lat = jnp.where(used, cell % 64, 64).astype(F32)
        rest = jnp.where(
            lax.broadcasted_iota(I32, (LANES - levels - 2 * foot, block), 0) == 0, 1.0, 0.0
        )
        payload = jnp.concatenate([share, jnp.concatenate([lon, lat], axis=0), rest], axis=0)
        pay_ref[cols, :] = payload.T
    even_ref[...] = jnp.zeros_like(even_ref)
    odd_ref[...] = jnp.zeros_like(odd_ref)
    copy.wait()
    unroll = 16

    def move(c, _):
        for u in range(unroll):
            slot = slot_s[c * unroll + u]
            to_ref = odd_ref if u % 2 else even_ref
            to_ref[pl.ds(slot, 1), :] = pay_ref[pl.ds(c * unroll + u, 1), :]
        return 0

    lax.fori_loop(0, (n_live + unroll - 1) // unroll, move, 0)
    out_ref[...] = (even_ref[:slots, :] + odd_ref[:slots, :]).astype(BF16)


def spread_kernel(
    capacity,
    lon_dev,
    lat_dev,
    levels,
    got_hbm,
    back_ref,
    mix_ref,
    out_hbm,
    got_ref,
    out_ref,
    share_ref,
    fields_v,
    meta_v,
    sems,
    got_sems,
    out_sems,
    *held,
):
    accs, tables = held[:N_ACC], held[N_ACC:]
    slots = got_ref.shape[0]
    ndev = slots // capacity
    ncells = lon_dev * lat_dev
    foot = 4
    load = pltpu.make_async_copy(back_ref, accs[0].at[pl.ds(0, ncells), :], sems.at[0])
    load.start()
    n_gets = 4
    piece = slots // n_gets
    gets = []
    for i in range(n_gets):
        at = pl.ds(i * piece, piece)
        get = pltpu.make_async_copy(got_hbm.at[at, :], got_ref.at[at, :], got_sems.at[i])
        get.start()
        gets.append(get)
    for acc in accs[1:]:
        acc[...] = jnp.zeros_like(acc)
    chunk = 8
    span = foot * chunk
    row_i = lax.broadcasted_iota(I32, (LANES, LANES), 0) - levels
    lane_i = lax.broadcasted_iota(I32, (LANES, LANES), 1)
    pick = (row_i >= 0) & (row_i <= 2 * foot) & (row_i == lane_i // chunk)
    pick = jnp.where(pick, 1.0, 0.0).astype(BF16)
    block = 256
    own = lax.broadcasted_iota(I32, (block, LANES), 0) % chunk
    own = own == lax.broadcasted_iota(I32, (block, LANES), 1) % chunk
    chunk_i = lax.broadcasted_iota(I32, (block // chunk, block), 0)
    gather = chunk_i == lax.broadcasted_iota(I32, (block // chunk, block), 1) // chunk
    gather = jnp.where(gather, 1.0, 0.0).astype(BF16)
    is_cell = lax.broadcasted_iota(I32, (block // chunk, LANES), 1) < span
    for b in range(slots // block):
        if b * block % piece == 0:
            gets[b * block // piece].wait()
        rows = slice(b * block, (b + 1) * block)
        part = got_ref[rows, :]
        fields = jnp.dot(part, pick, preferred_element_type=F32)
        fields = jnp.where(own, fields, 0.0).astype(BF16)
        table = jnp.dot(gather, fields, preferred_element_type=F32)
        turned = pltpu.roll(table, LANES - span, 1)
        table = jnp.where(is_cell, table + turned * float(lon_dev), table)
        at = b * (block // chunk)
        fields_v[at : at + block // chunk, :] = table
    lanes = list(range(span)) + [2 * span]
    for i in range(slots // chunk // LANES):
        cols = slice(i * LANES, (i + 1) * LANES)
        turned = fields_v[cols, :].T.astype(I32)
        for k, lane in enumerate(lanes):
            meta_v[k, :, cols] = turned[lane : lane + 1, :]
    copies = [pltpu.make_async_copy(meta_v.at[k, 0], t, sems.at[k + 1]) for k, t in enumerate(tables)]
    for copy in copies:
        copy.start()
    share_ref[...] = got_ref[...].astype(F32)
    load.wait()
    for copy in copies:
        copy.wait()
    per_source = capacity // chunk

    def one_source(s, _):
        base = s * per_source
        n_chunks = tables[span][base]
        for c in range(1, per_source):
            n_chunks = n_chunks + tables[span][base + c]

        def one_chunk(c, _):
            first = pl.multiple_of(c * chunk, chunk)
            for u in range(chunk):
                row = share_ref[pl.ds(first + u, 1), :]
                for f in range(foot):
                    cell = tables[f * chunk + u][c]
                    acc = accs[(u * foot + f) % N_ACC]
                    acc[pl.ds(cell, 1), :] = acc[pl.ds(cell, 1), :] + row
            return 0

        lax.fori_loop(base, base + n_chunks, one_chunk, 0)
        return 0

    lax.fori_loop(0, ndev, one_source, 0)
    lane = lax.broadcasted_iota(I32, (lon_dev, LANES), 1)

    puts = []
    for t in range(ncells // (4 * lon_dev)):
        rows = pl.ds(t * 4 * lon_dev, 4 * lon_dev)
        sums = [acc[rows, :] for acc in accs]
        while len(sums) > 1:
            sums = [a + b for a, b in zip(sums[::2], sums[1::2])]
        total = sums[0]
        high, low = split(total)
        both = jnp.dot(
            jnp.concatenate([high, low], axis=1), mix_ref[...], preferred_element_type=F32
        )
        mixed = both[:, :LANES] + both[:, LANES:]
        a = [mixed[j * lon_dev : (j + 1) * lon_dev, :] for j in range(4)]
        r1 = pltpu.roll(a[1], 96, 1)
        r2 = pltpu.roll(a[2], 64, 1)
        r3 = pltpu.roll(a[3], 32, 1)
        tiles = [
            jnp.where(lane < 96, a[0], r1),
            jnp.where(lane < 64, r1, r2),
            jnp.where(lane < 32, r2, r3),
        ]
        quantise(tiles, out_ref, t)
        put = pltpu.make_async_copy(out_ref.at[t], out_hbm.at[t], out_sems.at[t])
        put.start()
        puts.append(put)
    for put in puts:
        put.wait()


def prepare_kernel(lat_dev, back_ref, vert_ref, out_ref, mix_ref):
    ncells, levels = back_ref.shape
    lon_dev = ncells // lat_dev
    v_high, v_low = split(vert_ref[...].T)
    mix_ref[...] = jnp.zeros_like(mix_ref)
    mix_ref[:levels, :levels] = v_high
    mix_ref[:levels, LANES : LANES + levels] = v_low
    mix_ref[LANES : LANES + levels, :levels] = v_high
    out_ref[...] = jnp.zeros_like(out_ref)
    for lat in range(lat_dev):
        out_ref[lat * lon_dev : (lat + 1) * lon_dev, :levels] = back_ref[
            pl.ds(lat, lon_dev, stride=lat_dev), :
        ]


def toeplitz_kernel(kern_ref, ph_ref, pl_ref, mh_ref, ml_ref):
    n = kern_ref.shape[1]
    block = 256
    for high_ref, low_ref, row, sign in ((ph_ref, pl_ref, 0, False), (mh_ref, ml_ref, 1, True)):
        base = jnp.broadcast_to(kern_ref[row : row + 1, :], (block, n))
        strip = pltpu.roll(base, 0, 1, stride=1, stride_axis=0)
        for i in range(n // block):
            if i:
                strip = jnp.concatenate([strip[:, n - block :], strip[:, : n - block]], axis=1)
            piece = strip
            if sign:
                row_i = lax.broadcasted_iota(I32, (block, n), 0) + i * block
                piece = jnp.where(lax.broadcasted_iota(I32, (block, n), 1) > row_i, -strip, strip)
            high, low = split(piece)
            high_ref[i * block : (i + 1) * block, :] = high
            low_ref[i * block : (i + 1) * block, :] = low


def conv_kernel(*refs):
    got_hbm, mats, out_hbm = refs[0], refs[1:5], refs[5]
    got_ref, held, (xp, xm, yp, ym, out_ref, in_sems, mat_sems, out_sems) = (
        refs[6],
        refs[7:11],
        refs[11:],
    )
    n_lon = got_ref.shape[0]
    rows = got_ref.shape[1] - CODE_ROWS
    width = got_ref.shape[2]
    half = n_lon // 2
    gets = [
        pltpu.make_async_copy(got_hbm.at[s], got_ref.at[s], in_sems.at[s]) for s in range(n_lon)
    ]
    for s in range(half):
        gets[s].start()
        gets[s + half].start()
    loads = [pltpu.make_async_copy(a, b, mat_sems.at[i]) for i, (a, b) in enumerate(zip(mats, held))]
    for load in loads:
        load.start()
    ph_ref, pl_ref, mh_ref, ml_ref = held
    for s in range(half):
        gets[s].wait()
        gets[s + half].wait()
        a = dequantise(got_ref, s)
        b = dequantise(got_ref, s + half)
        at = slice(s * rows, (s + 1) * rows)
        xp[at, :width], xp[at, width:] = split(a + b)
        xm[at, :width], xm[at, width:] = split(a - b)
    for i, (th, tl, x, y) in enumerate(((ph_ref, pl_ref, xp, yp), (mh_ref, ml_ref, xm, ym))):
        loads[2 * i].wait()
        loads[2 * i + 1].wait()
        both = jnp.dot(th[...], x[...], preferred_element_type=F32)
        rest = jnp.dot(tl[...], x[:, :width], preferred_element_type=F32)
        y[...] = both[:, :width] + (both[:, width:] + rest)
    puts = []
    for s in range(half):
        at = slice(s * rows, (s + 1) * rows)
        plus, minus = yp[at, :], ym[at, :]
        for place, y in ((s, 0.5 * (plus + minus)), (s + half, 0.5 * (plus - minus))):
            quantise([y[:, k : k + LANES] for k in range(0, width, LANES)], out_ref, place)
            put = pltpu.make_async_copy(out_ref.at[place], out_hbm.at[place], out_sems.at[place])
            put.start()
            puts.append(put)
    for put in puts:
        put.wait()


def unpack_kernel(got_ref, out_ref, held_ref):
    lon_dev, lats, levels = out_ref.shape
    lane = lax.broadcasted_iota(I32, (lon_dev, LANES), 1)
    for t in range(got_ref.shape[0]):
        x = dequantise(got_ref, t)
        o = [x[:, k * LANES : (k + 1) * LANES] for k in range(3)]
        a = [
            o[0],
            pltpu.roll(jnp.where(lane >= 96, o[0], o[1]), 32, 1),
            pltpu.roll(jnp.where(lane >= 64, o[1], o[2]), 64, 1),
            pltpu.roll(o[2], 96, 1),
        ]
        for j in range(4):
            at = (t * 4 + j) * lon_dev
            held_ref[at : at + lon_dev, :] = a[j]
    for i in range(lon_dev):
        for g in range(0, lats, 8):
            picked = held_ref[pl.ds(g * lon_dev + i, 8, stride=lon_dev), :]
            out_ref[i, g : g + 8, :] = picked[:, :levels]


def call_spread(got, ordered, mixer, capacity, lon_dev, lat_dev, levels, coded):
    slots = got.shape[0]
    ncells = lon_dev * lat_dev
    acc = pltpu.VMEM((ncells + 8, LANES), F32)
    return pl.pallas_call(
        lambda *refs: spread_kernel(capacity, lon_dev, lat_dev, levels, *refs),
        out_shape=jax.ShapeDtypeStruct(coded, I16),
        in_specs=[pl.BlockSpec(memory_space=pl.ANY)] * 2 + vmem(1),
        out_specs=pl.BlockSpec(memory_space=pl.ANY),
        scratch_shapes=[
            pltpu.VMEM((slots, LANES), BF16),
            pltpu.VMEM(coded, I16),
            pltpu.VMEM((slots, LANES), F32),
            pltpu.VMEM((slots // 8, LANES), F32),
            pltpu.VMEM((33, 1, slots // 8), I32),
            pltpu.SemaphoreType.DMA((34,)),
            pltpu.SemaphoreType.DMA((4,)),
            pltpu.SemaphoreType.DMA((coded[0],)),
        ]
        + [acc] * N_ACC
        + [pltpu.SMEM((slots // 8,), I32)] * 33,
        compiler_params=params(),
        name="spread",
    )(got, ordered, mixer)


def call_convolve(columns, toeplitz, half, width, coded):
    part = pltpu.VMEM((half, 2 * width), BF16)
    wide = pltpu.VMEM((half, width), F32)
    n_lon = coded[0]
    anywhere = pl.BlockSpec(memory_space=pl.ANY)
    return pl.pallas_call(
        conv_kernel,
        out_shape=jax.ShapeDtypeStruct(coded, I16),
        in_specs=[anywhere] * 5,
        out_specs=anywhere,
        scratch_shapes=[pltpu.VMEM(coded, I16)]
        + [pltpu.VMEM((half, half), BF16)] * 4
        + [part] * 2
        + [wide] * 2
        + [
            pltpu.VMEM(coded, I16),
            pltpu.SemaphoreType.DMA((n_lon,)),
            pltpu.SemaphoreType.DMA((4,)),
            pltpu.SemaphoreType.DMA((n_lon,)),
        ],
        compiler_params=params(),
        name="convolve",
    )(columns, *toeplitz)


def call_unpack(back, lon_dev, lat_dev, levels, coded):
    n_lon = coded[0]
    return pl.pallas_call(
        unpack_kernel,
        grid=(n_lon // 4,),
        out_shape=jax.ShapeDtypeStruct((lon_dev, lat_dev, levels), F32),
        in_specs=[pl.BlockSpec((4,) + coded[1:], lambda g: (g, 0, 0))],
        out_specs=pl.BlockSpec((lon_dev, 16, levels), lambda g: (0, g, 0)),
        scratch_shapes=[pltpu.VMEM((16 * lon_dev, LANES), F32)],
        compiler_params=params(),
        name="unpack",
    )(back)


def per_device(
    radiances,
    owner_id,
    cell_index,
    valid_count,
    row_counts,
    jacobian,
    background,
    vertical,
    lon_kernel,
):
    n_lon = lax.axis_size("lon")
    ndev = n_lon * lax.axis_size("lat")
    nrows = radiances.shape[0]
    lon_dev, lat_dev, levels = background.shape
    capacity = 5 * nrows // (2 * ndev)
    slots = ndev * capacity
    ncells = lon_dev * lat_dev
    width = ncells // n_lon // lon_dev * levels
    coded = (n_lon, lon_dev + CODE_ROWS, width)

    sent = pl.pallas_call(
        lambda *refs: dispatch_kernel(capacity, *refs),
        out_shape=jax.ShapeDtypeStruct((slots, LANES), BF16),
        in_specs=[pl.BlockSpec(memory_space=pltpu.SMEM)] + vmem(5),
        out_specs=vmem(1)[0],
        scratch_shapes=[
            pltpu.VMEM((nrows, LANES), F32),
            pltpu.VMEM((slots + 8, LANES), F32),
            pltpu.VMEM((slots + 8, LANES), F32),
            pltpu.VMEM((1, nrows), I32),
            pltpu.SMEM((nrows,), I32),
            pltpu.SemaphoreType.DMA,
        ],
        compiler_params=params(),
        name="dispatch",
    )(
        row_counts,
        radiances,
        owner_id.T,
        cell_index.T,
        valid_count.reshape(1, nrows),
        jacobian.T,
    )
    sent, background, vertical = lax.optimization_barrier((sent, background, vertical))
    got = lax.all_to_all(
        sent.reshape(ndev, capacity, LANES), ("lon", "lat"), split_axis=0, concat_axis=0, tiled=True
    ).reshape(slots, LANES)
    ordered, mixer = pl.pallas_call(
        lambda *refs: prepare_kernel(lat_dev, *refs),
        out_shape=(
            jax.ShapeDtypeStruct((ncells, LANES), F32),
            jax.ShapeDtypeStruct((2 * LANES, 2 * LANES), BF16),
        ),
        in_specs=vmem(2),
        out_specs=tuple(vmem(2)),
        compiler_params=params(63),
        cost_estimate=pl.CostEstimate(flops=0, bytes_accessed=12_000_000, transcendentals=0),
        name="prepare",
    )(background.reshape(ncells, levels), vertical)
    field = call_spread(got, ordered, mixer, capacity, lon_dev, lat_dev, levels, coded)

    half = n_lon * lon_dev // 2
    turned_kernel = jnp.roll(lon_kernel[::-1], 1)
    plus = turned_kernel[:half] + turned_kernel[half:]
    minus = turned_kernel[half:] - turned_kernel[:half]
    first = lon_kernel[:half] - lon_kernel[half:]
    minus = jnp.roll(first[::-1], 1)
    square = jax.ShapeDtypeStruct((half, half), BF16)
    toeplitz = pl.pallas_call(
        toeplitz_kernel,
        out_shape=(square,) * 4,
        in_specs=vmem(1),
        out_specs=tuple(vmem(4)),
        compiler_params=params(63),
        name="toeplitz",
    )(jnp.stack([plus, minus]))

    columns = lax.all_to_all(field, "lon", split_axis=0, concat_axis=0, tiled=True)
    result = call_convolve(columns, toeplitz, half, width, coded)
    back = lax.all_to_all(result, "lon", split_axis=0, concat_axis=0, tiled=True)
    return call_unpack(back, lon_dev, lat_dev, levels, coded)


def solution(mesh):
    return jax.shard_map(
        per_device,
        mesh=mesh,
        in_specs=(
            P(("lon", "lat"), None),
            P(("lon", "lat"), None),
            P(("lon", "lat"), None),
            P(("lon", "lat")),
            P(("lon", "lat")),
            P(),
            P("lon", "lat", None),
            P(),
            P(),
        ),
        out_specs=P("lon", "lat", None),
        check_vma=False,
    )
```

```python
import jax
import jax.numpy as jnp
from jax import lax
from jax.experimental import pallas as pl
from jax.experimental.pallas import tpu as pltpu
from jax.sharding import PartitionSpec as P

F32 = jnp.float32
BF16 = jnp.bfloat16
I32 = jnp.int32
I16 = jnp.int16
LANES = 128
N_ACC = 8
TOP = 32700.0
LOWEST = -110.0
CODE_ROWS = 8


def vmem(n):
    return [pl.BlockSpec(memory_space=pltpu.VMEM)] * n


def params(mib=56):
    return pltpu.CompilerParams(vmem_limit_bytes=mib * 1024 * 1024)


def quantise(tiles, out_ref, place):
    rows = tiles[0].shape[0]
    for k, tile in enumerate(tiles):
        top = jnp.max(jnp.abs(tile), axis=0, keepdims=True)
        power = jnp.maximum(jnp.ceil(jnp.log2(top)), LOWEST)
        factor = jnp.exp2(-power) * TOP
        digits = jnp.round(tile * factor)
        codes = jnp.broadcast_to(power, (CODE_ROWS, LANES))
        whole = jnp.concatenate([digits, codes], axis=0).astype(I32)
        out_ref[place, :, k * LANES : (k + 1) * LANES] = whole.astype(I16)


def dequantise(in_ref, place):
    whole = in_ref[place].astype(I32).astype(F32)
    rows = whole.shape[0] - CODE_ROWS
    factor = jnp.exp2(whole[rows : rows + 1]) * (1.0 / TOP)
    return whole[:rows] * factor


def split(x):
    high = x.astype(BF16)
    low = (x - high.astype(F32)).astype(BF16)
    return high, low


def dispatch_kernel(
    capacity,
    live_ref,
    rad_ref,
    owner_ref,
    cell_ref,
    count_ref,
    jac_ref,
    out_ref,
    pay_ref,
    even_ref,
    odd_ref,
    slot_v,
    slot_s,
    sem,
):
    nrows = rad_ref.shape[0]
    levels = jac_ref.shape[0]
    slots = out_ref.shape[0]
    ndev = slots // capacity
    foot = cell_ref.shape[0]
    n_live = live_ref[0]
    block = 256
    owner_ids = lax.broadcasted_iota(I32, (ndev, block), 0)
    earlier = (
        lax.broadcasted_iota(I32, (block, block), 0) < lax.broadcasted_iota(I32, (block, block), 1)
    ).astype(F32).astype(BF16)
    carry = jnp.zeros((ndev, 1), F32)
    for b in range(nrows // block):
        cols = slice(b * block, (b + 1) * block)
        position = lax.broadcasted_iota(I32, (1, block), 1) + b * block
        live = position < n_live
        owner = owner_ref[:, cols]
        hit = ((owner_ids == owner) & live).astype(F32)
        before = jnp.dot(hit.astype(BF16), earlier, preferred_element_type=F32) + carry
        rank = jnp.sum(hit * before, axis=0, keepdims=True).astype(I32)
        carry = carry + jnp.sum(hit, axis=1, keepdims=True)
        slot = jnp.where(live, owner * capacity + rank, slots)
        for i in range(block // LANES):
            row = b * (block // LANES) + i
            slot_v[:, row * LANES : (row + 1) * LANES] = slot[:, i * LANES : (i + 1) * LANES]
    copy = pltpu.make_async_copy(slot_v.at[0], slot_s, sem)
    copy.start()
    for b in range(nrows // block):
        cols = slice(b * block, (b + 1) * block)
        profile = lax.dot_general(
            jac_ref[...], rad_ref[cols, :], (((1,), (1,)), ((), ())), preferred_element_type=F32
        )
        count = count_ref[:, cols]
        share = (profile * (1.0 / count.astype(F32))).astype(BF16).astype(F32)
        cell = cell_ref[:, cols]
        used = lax.broadcasted_iota(I32, (foot, block), 0) < count
        lon = jnp.where(used, cell // 64, 0).astype(F32)
        lat = jnp.where(used, cell % 64, 64).astype(F32)
        rest = jnp.where(
            lax.broadcasted_iota(I32, (LANES - levels - 2 * foot, block), 0) == 0, 1.0, 0.0
        )
        payload = jnp.concatenate([share, jnp.concatenate([lon, lat], axis=0), rest], axis=0)
        pay_ref[cols, :] = payload.T
    even_ref[...] = jnp.zeros_like(even_ref)
    odd_ref[...] = jnp.zeros_like(odd_ref)
    copy.wait()
    unroll = 16

    def move(c, _):
        for u in range(unroll):
            slot = slot_s[c * unroll + u]
            to_ref = odd_ref if u % 2 else even_ref
            to_ref[pl.ds(slot, 1), :] = pay_ref[pl.ds(c * unroll + u, 1), :]
        return 0

    lax.fori_loop(0, (n_live + unroll - 1) // unroll, move, 0)
    out_ref[...] = (even_ref[:slots, :] + odd_ref[:slots, :]).astype(BF16)


def spread_kernel(
    capacity,
    lon_dev,
    lat_dev,
    levels,
    got_hbm,
    back_ref,
    mix_ref,
    out_hbm,
    got_ref,
    out_ref,
    share_ref,
    fields_v,
    meta_v,
    sems,
    got_sems,
    out_sems,
    *held,
):
    accs, tables = held[:N_ACC], held[N_ACC:]
    slots = got_ref.shape[0]
    ndev = slots // capacity
    ncells = lon_dev * lat_dev
    foot = 4
    load = pltpu.make_async_copy(back_ref, accs[0].at[pl.ds(0, ncells), :], sems.at[0])
    load.start()
    n_gets = 4
    piece = slots // n_gets
    gets = []
    for i in range(n_gets):
        at = pl.ds(i * piece, piece)
        get = pltpu.make_async_copy(got_hbm.at[at, :], got_ref.at[at, :], got_sems.at[i])
        get.start()
        gets.append(get)
    for acc in accs[1:]:
        acc[...] = jnp.zeros_like(acc)
    chunk = 8
    span = foot * chunk
    row_i = lax.broadcasted_iota(I32, (LANES, LANES), 0) - levels
    lane_i = lax.broadcasted_iota(I32, (LANES, LANES), 1)
    pick = (row_i >= 0) & (row_i <= 2 * foot) & (row_i == lane_i // chunk)
    pick = jnp.where(pick, 1.0, 0.0).astype(BF16)
    block = 256
    own = lax.broadcasted_iota(I32, (block, LANES), 0) % chunk
    own = own == lax.broadcasted_iota(I32, (block, LANES), 1) % chunk
    chunk_i = lax.broadcasted_iota(I32, (block // chunk, block), 0)
    gather = chunk_i == lax.broadcasted_iota(I32, (block // chunk, block), 1) // chunk
    gather = jnp.where(gather, 1.0, 0.0).astype(BF16)
    is_cell = lax.broadcasted_iota(I32, (block // chunk, LANES), 1) < span
    for b in range(slots // block):
        if b * block % piece == 0:
            gets[b * block // piece].wait()
        rows = slice(b * block, (b + 1) * block)
        part = got_ref[rows, :]
        fields = jnp.dot(part, pick, preferred_element_type=F32)
        fields = jnp.where(own, fields, 0.0).astype(BF16)
        table = jnp.dot(gather, fields, preferred_element_type=F32)
        turned = pltpu.roll(table, LANES - span, 1)
        table = jnp.where(is_cell, table + turned * float(lon_dev), table)
        at = b * (block // chunk)
        fields_v[at : at + block // chunk, :] = table
    lanes = list(range(span)) + [2 * span]
    for i in range(slots // chunk // LANES):
        cols = slice(i * LANES, (i + 1) * LANES)
        turned = fields_v[cols, :].T.astype(I32)
        for k, lane in enumerate(lanes):
            meta_v[k, :, cols] = turned[lane : lane + 1, :]
    copies = [pltpu.make_async_copy(meta_v.at[k, 0], t, sems.at[k + 1]) for k, t in enumerate(tables)]
    for copy in copies:
        copy.start()
    share_ref[...] = got_ref[...].astype(F32)
    load.wait()
    for copy in copies:
        copy.wait()
    per_source = capacity // chunk

    def one_source(s, _):
        base = s * per_source
        n_chunks = tables[span][base]
        for c in range(1, per_source):
            n_chunks = n_chunks + tables[span][base + c]

        def one_chunk(c, _):
            first = pl.multiple_of(c * chunk, chunk)
            for u in range(chunk):
                row = share_ref[pl.ds(first + u, 1), :]
                for f in range(foot):
                    cell = tables[f * chunk + u][c]
                    acc = accs[(u * foot + f) % N_ACC]
                    acc[pl.ds(cell, 1), :] = acc[pl.ds(cell, 1), :] + row
            return 0

        lax.fori_loop(base, base + n_chunks, one_chunk, 0)
        return 0

    lax.fori_loop(0, ndev, one_source, 0)
    lane = lax.broadcasted_iota(I32, (lon_dev, LANES), 1)

    puts = []
    for t in range(ncells // (4 * lon_dev)):
        rows = pl.ds(t * 4 * lon_dev, 4 * lon_dev)
        sums = [acc[rows, :] for acc in accs]
        while len(sums) > 1:
            sums = [a + b for a, b in zip(sums[::2], sums[1::2])]
        total = sums[0]
        high, low = split(total)
        both = jnp.dot(
            jnp.concatenate([high, low], axis=1), mix_ref[...], preferred_element_type=F32
        )
        mixed = both[:, :LANES] + both[:, LANES:]
        a = [mixed[j * lon_dev : (j + 1) * lon_dev, :] for j in range(4)]
        r1 = pltpu.roll(a[1], 96, 1)
        r2 = pltpu.roll(a[2], 64, 1)
        r3 = pltpu.roll(a[3], 32, 1)
        tiles = [
            jnp.where(lane < 96, a[0], r1),
            jnp.where(lane < 64, r1, r2),
            jnp.where(lane < 32, r2, r3),
        ]
        quantise(tiles, out_ref, t)
        put = pltpu.make_async_copy(out_ref.at[t], out_hbm.at[t], out_sems.at[t])
        put.start()
        puts.append(put)
    for put in puts:
        put.wait()


def prepare_kernel(lat_dev, back_ref, vert_ref, out_ref, mix_ref):
    ncells, levels = back_ref.shape
    lon_dev = ncells // lat_dev
    v_high, v_low = split(vert_ref[...].T)
    mix_ref[...] = jnp.zeros_like(mix_ref)
    mix_ref[:levels, :levels] = v_high
    mix_ref[:levels, LANES : LANES + levels] = v_low
    mix_ref[LANES : LANES + levels, :levels] = v_high
    out_ref[...] = jnp.zeros_like(out_ref)
    for lat in range(lat_dev):
        out_ref[lat * lon_dev : (lat + 1) * lon_dev, :levels] = back_ref[
            pl.ds(lat, lon_dev, stride=lat_dev), :
        ]


def toeplitz_kernel(kern_ref, ph_ref, pl_ref, mh_ref, ml_ref):
    n = kern_ref.shape[1]
    block = 256
    for high_ref, low_ref, row, sign in ((ph_ref, pl_ref, 0, False), (mh_ref, ml_ref, 1, True)):
        base = jnp.broadcast_to(kern_ref[row : row + 1, :], (block, n))
        strip = pltpu.roll(base, 0, 1, stride=1, stride_axis=0)
        for i in range(n // block):
            if i:
                strip = jnp.concatenate([strip[:, n - block :], strip[:, : n - block]], axis=1)
            piece = strip
            if sign:
                row_i = lax.broadcasted_iota(I32, (block, n), 0) + i * block
                piece = jnp.where(lax.broadcasted_iota(I32, (block, n), 1) > row_i, -strip, strip)
            high, low = split(piece)
            high_ref[i * block : (i + 1) * block, :] = high
            low_ref[i * block : (i + 1) * block, :] = low


def conv_kernel(*refs):
    got_hbm, mats, out_hbm = refs[0], refs[1:5], refs[5]
    got_ref, held, (xp, xm, yp, ym, out_ref, in_sems, mat_sems, out_sems) = (
        refs[6],
        refs[7:11],
        refs[11:],
    )
    n_lon = got_ref.shape[0]
    rows = got_ref.shape[1] - CODE_ROWS
    width = got_ref.shape[2]
    half = n_lon // 2
    gets = [
        pltpu.make_async_copy(got_hbm.at[s], got_ref.at[s], in_sems.at[s]) for s in range(n_lon)
    ]
    for s in range(half):
        gets[s].start()
        gets[s + half].start()
    loads = [pltpu.make_async_copy(a, b, mat_sems.at[i]) for i, (a, b) in enumerate(zip(mats, held))]
    for load in loads:
        load.start()
    ph_ref, pl_ref, mh_ref, ml_ref = held
    for s in range(half):
        gets[s].wait()
        gets[s + half].wait()
        a = dequantise(got_ref, s)
        b = dequantise(got_ref, s + half)
        at = slice(s * rows, (s + 1) * rows)
        xp[at, :width], xp[at, width:] = split(a + b)
        xm[at, :width], xm[at, width:] = split(a - b)
    for i, (th, tl, x, y) in enumerate(((ph_ref, pl_ref, xp, yp), (mh_ref, ml_ref, xm, ym))):
        loads[2 * i].wait()
        loads[2 * i + 1].wait()
        both = jnp.dot(th[...], x[...], preferred_element_type=F32)
        rest = jnp.dot(tl[...], x[:, :width], preferred_element_type=F32)
        y[...] = both[:, :width] + (both[:, width:] + rest)
    puts = []
    for s in range(half):
        at = slice(s * rows, (s + 1) * rows)
        plus, minus = yp[at, :], ym[at, :]
        for place, y in ((s, 0.5 * (plus + minus)), (s + half, 0.5 * (plus - minus))):
            quantise([y[:, k : k + LANES] for k in range(0, width, LANES)], out_ref, place)
            put = pltpu.make_async_copy(out_ref.at[place], out_hbm.at[place], out_sems.at[place])
            put.start()
            puts.append(put)
    for put in puts:
        put.wait()


def unpack_kernel(got_ref, out_ref, held_ref):
    lon_dev, lats, levels = out_ref.shape
    lane = lax.broadcasted_iota(I32, (lon_dev, LANES), 1)
    for t in range(got_ref.shape[0]):
        x = dequantise(got_ref, t)
        o = [x[:, k * LANES : (k + 1) * LANES] for k in range(3)]
        a = [
            o[0],
            pltpu.roll(jnp.where(lane >= 96, o[0], o[1]), 32, 1),
            pltpu.roll(jnp.where(lane >= 64, o[1], o[2]), 64, 1),
            pltpu.roll(o[2], 96, 1),
        ]
        for j in range(4):
            at = (t * 4 + j) * lon_dev
            held_ref[at : at + lon_dev, :] = a[j]
    row = lax.broadcasted_iota(I32, (8, LANES), 0)
    for i in range(0, lon_dev, 8):
        for g in range(0, lats, 8):
            square = [held_ref[(g + j) * lon_dev + i : (g + j) * lon_dev + i + 8, :] for j in range(8)]
            for n, line in enumerate(transpose8(square, row)):
                out_ref[i + n, g : g + 8, :] = line[:, :levels]


def transpose8(square, row):
    for step in (4, 2, 1):
        low = (row & step) == 0
        turned = list(square)
        for j in range(8):
            if j & step:
                continue
            a, b = square[j], square[j + step]
            turned[j] = jnp.where(low, a, pltpu.roll(b, step, 0))
            turned[j + step] = jnp.where(low, pltpu.roll(a, 8 - step, 0), b)
        square = turned
    return square


def call_spread(got, ordered, mixer, capacity, lon_dev, lat_dev, levels, coded):
    slots = got.shape[0]
    ncells = lon_dev * lat_dev
    acc = pltpu.VMEM((ncells + 8, LANES), F32)
    return pl.pallas_call(
        lambda *refs: spread_kernel(capacity, lon_dev, lat_dev, levels, *refs),
        out_shape=jax.ShapeDtypeStruct(coded, I16),
        in_specs=[pl.BlockSpec(memory_space=pl.ANY)] * 2 + vmem(1),
        out_specs=pl.BlockSpec(memory_space=pl.ANY),
        scratch_shapes=[
            pltpu.VMEM((slots, LANES), BF16),
            pltpu.VMEM(coded, I16),
            pltpu.VMEM((slots, LANES), F32),
            pltpu.VMEM((slots // 8, LANES), F32),
            pltpu.VMEM((33, 1, slots // 8), I32),
            pltpu.SemaphoreType.DMA((34,)),
            pltpu.SemaphoreType.DMA((4,)),
            pltpu.SemaphoreType.DMA((coded[0],)),
        ]
        + [acc] * N_ACC
        + [pltpu.SMEM((slots // 8,), I32)] * 33,
        compiler_params=params(),
        name="spread",
    )(got, ordered, mixer)


def call_convolve(columns, toeplitz, half, width, coded):
    part = pltpu.VMEM((half, 2 * width), BF16)
    wide = pltpu.VMEM((half, width), F32)
    n_lon = coded[0]
    anywhere = pl.BlockSpec(memory_space=pl.ANY)
    return pl.pallas_call(
        conv_kernel,
        out_shape=jax.ShapeDtypeStruct(coded, I16),
        in_specs=[anywhere] * 5,
        out_specs=anywhere,
        scratch_shapes=[pltpu.VMEM(coded, I16)]
        + [pltpu.VMEM((half, half), BF16)] * 4
        + [part] * 2
        + [wide] * 2
        + [
            pltpu.VMEM(coded, I16),
            pltpu.SemaphoreType.DMA((n_lon,)),
            pltpu.SemaphoreType.DMA((4,)),
            pltpu.SemaphoreType.DMA((n_lon,)),
        ],
        compiler_params=params(),
        name="convolve",
    )(columns, *toeplitz)


def call_unpack(back, lon_dev, lat_dev, levels, coded):
    n_lon = coded[0]
    return pl.pallas_call(
        unpack_kernel,
        grid=(n_lon // 4,),
        out_shape=jax.ShapeDtypeStruct((lon_dev, lat_dev, levels), F32),
        in_specs=[pl.BlockSpec((4,) + coded[1:], lambda g: (g, 0, 0))],
        out_specs=pl.BlockSpec((lon_dev, 16, levels), lambda g: (0, g, 0)),
        scratch_shapes=[pltpu.VMEM((16 * lon_dev, LANES), F32)],
        compiler_params=params(),
        name="unpack",
    )(back)


def per_device(
    radiances,
    owner_id,
    cell_index,
    valid_count,
    row_counts,
    jacobian,
    background,
    vertical,
    lon_kernel,
):
    n_lon = lax.axis_size("lon")
    ndev = n_lon * lax.axis_size("lat")
    nrows = radiances.shape[0]
    lon_dev, lat_dev, levels = background.shape
    capacity = 5 * nrows // (2 * ndev)
    slots = ndev * capacity
    ncells = lon_dev * lat_dev
    width = ncells // n_lon // lon_dev * levels
    coded = (n_lon, lon_dev + CODE_ROWS, width)

    sent = pl.pallas_call(
        lambda *refs: dispatch_kernel(capacity, *refs),
        out_shape=jax.ShapeDtypeStruct((slots, LANES), BF16),
        in_specs=[pl.BlockSpec(memory_space=pltpu.SMEM)] + vmem(5),
        out_specs=vmem(1)[0],
        scratch_shapes=[
            pltpu.VMEM((nrows, LANES), F32),
            pltpu.VMEM((slots + 8, LANES), F32),
            pltpu.VMEM((slots + 8, LANES), F32),
            pltpu.VMEM((1, nrows), I32),
            pltpu.SMEM((nrows,), I32),
            pltpu.SemaphoreType.DMA,
        ],
        compiler_params=params(),
        name="dispatch",
    )(
        row_counts,
        radiances,
        owner_id.T,
        cell_index.T,
        valid_count.reshape(1, nrows),
        jacobian.T,
    )
    sent, background, vertical = lax.optimization_barrier((sent, background, vertical))
    got = lax.all_to_all(
        sent.reshape(ndev, capacity, LANES), ("lon", "lat"), split_axis=0, concat_axis=0, tiled=True
    ).reshape(slots, LANES)
    ordered, mixer = pl.pallas_call(
        lambda *refs: prepare_kernel(lat_dev, *refs),
        out_shape=(
            jax.ShapeDtypeStruct((ncells, LANES), F32),
            jax.ShapeDtypeStruct((2 * LANES, 2 * LANES), BF16),
        ),
        in_specs=vmem(2),
        out_specs=tuple(vmem(2)),
        compiler_params=params(63),
        cost_estimate=pl.CostEstimate(flops=0, bytes_accessed=12_000_000, transcendentals=0),
        name="prepare",
    )(background.reshape(ncells, levels), vertical)
    field = call_spread(got, ordered, mixer, capacity, lon_dev, lat_dev, levels, coded)

    half = n_lon * lon_dev // 2
    turned_kernel = jnp.roll(lon_kernel[::-1], 1)
    plus = turned_kernel[:half] + turned_kernel[half:]
    minus = turned_kernel[half:] - turned_kernel[:half]
    first = lon_kernel[:half] - lon_kernel[half:]
    minus = jnp.roll(first[::-1], 1)
    square = jax.ShapeDtypeStruct((half, half), BF16)
    toeplitz = pl.pallas_call(
        toeplitz_kernel,
        out_shape=(square,) * 4,
        in_specs=vmem(1),
        out_specs=tuple(vmem(4)),
        compiler_params=params(63),
        name="toeplitz",
    )(jnp.stack([plus, minus]))

    columns = lax.all_to_all(field, "lon", split_axis=0, concat_axis=0, tiled=True)
    result = call_convolve(columns, toeplitz, half, width, coded)
    back = lax.all_to_all(result, "lon", split_axis=0, concat_axis=0, tiled=True)
    return call_unpack(back, lon_dev, lat_dev, levels, coded)


def solution(mesh):
    return jax.shard_map(
        per_device,
        mesh=mesh,
        in_specs=(
            P(("lon", "lat"), None),
            P(("lon", "lat"), None),
            P(("lon", "lat"), None),
            P(("lon", "lat")),
            P(("lon", "lat")),
            P(),
            P("lon", "lat", None),
            P(),
            P(),
        ),
        out_specs=P("lon", "lat", None),
        check_vma=False,
    )
```

```python
import jax
import jax.numpy as jnp
from jax import lax
from jax.experimental import pallas as pl
from jax.experimental.pallas import tpu as pltpu
from jax.sharding import PartitionSpec as P

F32 = jnp.float32
BF16 = jnp.bfloat16
I32 = jnp.int32
I16 = jnp.int16
LANES = 128
N_ACC = 8
TOP = 32700.0
LOWEST = -110.0
CODE_ROWS = 8


def vmem(n):
    return [pl.BlockSpec(memory_space=pltpu.VMEM)] * n


def params(mib=56):
    return pltpu.CompilerParams(vmem_limit_bytes=mib * 1024 * 1024)


def quantise(tiles, out_ref, place):
    rows = tiles[0].shape[0]
    for k, tile in enumerate(tiles):
        top = jnp.max(jnp.abs(tile), axis=0, keepdims=True)
        power = jnp.maximum(jnp.ceil(jnp.log2(top)), LOWEST)
        factor = jnp.exp2(-power) * TOP
        digits = jnp.round(tile * factor)
        codes = jnp.broadcast_to(power, (CODE_ROWS, LANES))
        whole = jnp.concatenate([digits, codes], axis=0).astype(I32)
        out_ref[place, :, k * LANES : (k + 1) * LANES] = whole.astype(I16)


def dequantise(in_ref, place):
    whole = in_ref[place].astype(I32).astype(F32)
    rows = whole.shape[0] - CODE_ROWS
    factor = jnp.exp2(whole[rows : rows + 1]) * (1.0 / TOP)
    return whole[:rows] * factor


def split(x):
    high = x.astype(BF16)
    low = (x - high.astype(F32)).astype(BF16)
    return high, low


def dispatch_kernel(
    capacity,
    live_ref,
    rad_ref,
    owner_ref,
    cell_ref,
    count_ref,
    jac_ref,
    out_ref,
    pay_ref,
    even_ref,
    odd_ref,
    slot_v,
    slot_s,
    sem,
):
    nrows = rad_ref.shape[0]
    levels = jac_ref.shape[0]
    slots = out_ref.shape[0]
    ndev = slots // capacity
    foot = cell_ref.shape[0]
    n_live = live_ref[0]
    block = 256
    owner_ids = lax.broadcasted_iota(I32, (ndev, block), 0)
    earlier = (
        lax.broadcasted_iota(I32, (block, block), 0) < lax.broadcasted_iota(I32, (block, block), 1)
    ).astype(F32).astype(BF16)


    def hits(b):
        cols = slice(b * block, (b + 1) * block)
        position = lax.broadcasted_iota(I32, (1, block), 1) + b * block
        live = position < n_live
        owner = owner_ref[:, cols]
        hit = (owner_ids == owner) & live
        full = count_ref[:, cols] > 2
        return live, owner, (hit & full).astype(F32), (hit & ~full).astype(F32)

    full_carry = jnp.zeros((ndev, 1), F32)
    rest_carry = full_carry
    for b in range(nrows // block):
        rest_carry = rest_carry + jnp.sum(hits(b)[2], axis=1, keepdims=True)
    for b in range(nrows // block):
        live, owner, full, rest = hits(b)
        both = jnp.concatenate([full, rest], axis=0).astype(BF16)
        before = jnp.dot(both, earlier, preferred_element_type=F32)
        rank = full * (before[:ndev] + full_carry) + rest * (before[ndev:] + rest_carry)
        rank = jnp.sum(rank, axis=0, keepdims=True).astype(I32)
        full_carry = full_carry + jnp.sum(full, axis=1, keepdims=True)
        rest_carry = rest_carry + jnp.sum(rest, axis=1, keepdims=True)
        slot = jnp.where(live, owner * capacity + rank, slots)
        for i in range(block // LANES):
            row = b * (block // LANES) + i
            slot_v[:, row * LANES : (row + 1) * LANES] = slot[:, i * LANES : (i + 1) * LANES]
    copy = pltpu.make_async_copy(slot_v.at[0], slot_s, sem)
    copy.start()
    for b in range(nrows // block):
        cols = slice(b * block, (b + 1) * block)
        profile = lax.dot_general(
            jac_ref[...], rad_ref[cols, :], (((1,), (1,)), ((), ())), preferred_element_type=F32
        )
        count = count_ref[:, cols]
        share = (profile * (1.0 / count.astype(F32))).astype(BF16).astype(F32)
        cell = cell_ref[:, cols]
        used = lax.broadcasted_iota(I32, (foot, block), 0) < count
        lon = jnp.where(used, cell // 64, 0).astype(F32)
        lat = jnp.where(used, cell % 64, 64).astype(F32)
        kind = lax.broadcasted_iota(I32, (LANES - levels - 2 * foot, block), 0)
        rest = jnp.where((kind == 0) | ((kind == 1) & (count > 2)), 1.0, 0.0)
        payload = jnp.concatenate([share, jnp.concatenate([lon, lat], axis=0), rest], axis=0)
        pay_ref[cols, :] = payload.T
    even_ref[...] = jnp.zeros_like(even_ref)
    odd_ref[...] = jnp.zeros_like(odd_ref)
    copy.wait()
    unroll = 16

    def move(c, _):
        for u in range(unroll):
            slot = slot_s[c * unroll + u]
            to_ref = odd_ref if u % 2 else even_ref
            to_ref[pl.ds(slot, 1), :] = pay_ref[pl.ds(c * unroll + u, 1), :]
        return 0

    lax.fori_loop(0, (n_live + unroll - 1) // unroll, move, 0)
    out_ref[...] = (even_ref[:slots, :] + odd_ref[:slots, :]).astype(BF16)


def spread_kernel(
    capacity,
    lon_dev,
    lat_dev,
    levels,
    got_hbm,
    back_ref,
    mix_ref,
    out_hbm,
    got_ref,
    out_ref,
    share_ref,
    fields_v,
    meta_v,
    sems,
    got_sems,
    out_sems,
    *held,
):
    accs, tables = held[:N_ACC], held[N_ACC:]
    slots = got_ref.shape[0]
    ndev = slots // capacity
    ncells = lon_dev * lat_dev
    foot = 4
    load = pltpu.make_async_copy(back_ref, accs[0].at[pl.ds(0, ncells), :], sems.at[0])
    load.start()
    n_gets = 4
    piece = slots // n_gets
    gets = []
    for i in range(n_gets):
        at = pl.ds(i * piece, piece)
        get = pltpu.make_async_copy(got_hbm.at[at, :], got_ref.at[at, :], got_sems.at[i])
        get.start()
        gets.append(get)
    for acc in accs[1:]:
        acc[...] = jnp.zeros_like(acc)
    chunk = 8
    span = foot * chunk
    row_i = lax.broadcasted_iota(I32, (LANES, LANES), 0) - levels
    lane_i = lax.broadcasted_iota(I32, (LANES, LANES), 1)
    pick = (row_i >= 0) & (row_i <= 2 * foot + 1) & (row_i == lane_i // chunk)
    pick = jnp.where(pick, 1.0, 0.0).astype(BF16)
    block = 256
    own = lax.broadcasted_iota(I32, (block, LANES), 0) % chunk
    own = own == lax.broadcasted_iota(I32, (block, LANES), 1) % chunk
    chunk_i = lax.broadcasted_iota(I32, (block // chunk, block), 0)
    gather = chunk_i == lax.broadcasted_iota(I32, (block // chunk, block), 1) // chunk
    gather = jnp.where(gather, 1.0, 0.0).astype(BF16)
    is_cell = lax.broadcasted_iota(I32, (block // chunk, LANES), 1) < span
    for b in range(slots // block):
        if b * block % piece == 0:
            gets[b * block // piece].wait()
        rows = slice(b * block, (b + 1) * block)
        part = got_ref[rows, :]
        fields = jnp.dot(part, pick, preferred_element_type=F32)
        fields = jnp.where(own, fields, 0.0).astype(BF16)
        table = jnp.dot(gather, fields, preferred_element_type=F32)
        turned = pltpu.roll(table, LANES - span, 1)
        table = jnp.where(is_cell, table + turned * float(lon_dev), table)
        at = b * (block // chunk)
        fields_v[at : at + block // chunk, :] = table
    lanes = list(range(span)) + [2 * span, 2 * span + chunk]
    for i in range(slots // chunk // LANES):
        cols = slice(i * LANES, (i + 1) * LANES)
        turned = fields_v[cols, :].T.astype(I32)
        for k, lane in enumerate(lanes):
            meta_v[k, :, cols] = turned[lane : lane + 1, :]
    copies = [pltpu.make_async_copy(meta_v.at[k, 0], t, sems.at[k + 1]) for k, t in enumerate(tables)]
    for copy in copies:
        copy.start()
    share_ref[...] = got_ref[...].astype(F32)
    load.wait()
    for copy in copies:
        copy.wait()
    per_source = capacity // chunk

    def one_source(s, _):
        base = s * per_source
        n_chunks = tables[span][base]
        for c in range(1, per_source):
            n_chunks = n_chunks + tables[span][base + c]
        n_full = tables[span + 1][base]
        for c in range(1, per_source):
            n_full = n_full + tables[span + 1][base + c]

        def one_chunk(c, used):
            first = pl.multiple_of(c * chunk, chunk)
            for u in range(chunk):
                row = share_ref[pl.ds(first + u, 1), :]
                for f in range(used):
                    cell = tables[f * chunk + u][c]
                    acc = accs[(u * used + f) % N_ACC]
                    acc[pl.ds(cell, 1), :] = acc[pl.ds(cell, 1), :] + row

        def full_chunk(c, _):
            one_chunk(c, foot)
            return 0

        def half_chunk(c, _):
            one_chunk(c, foot // 2)
            return 0

        lax.fori_loop(base, base + n_full, full_chunk, 0)
        lax.fori_loop(base + n_full, base + n_chunks, half_chunk, 0)
        return 0

    lax.fori_loop(0, ndev, one_source, 0)
    lane = lax.broadcasted_iota(I32, (lon_dev, LANES), 1)

    puts = []
    for t in range(ncells // (4 * lon_dev)):
        rows = pl.ds(t * 4 * lon_dev, 4 * lon_dev)
        sums = [acc[rows, :] for acc in accs]
        while len(sums) > 1:
            sums = [a + b for a, b in zip(sums[::2], sums[1::2])]
        total = sums[0]
        high, low = split(total)
        both = jnp.dot(
            jnp.concatenate([high, low], axis=1), mix_ref[...], preferred_element_type=F32
        )
        mixed = both[:, :LANES] + both[:, LANES:]
        a = [mixed[j * lon_dev : (j + 1) * lon_dev, :] for j in range(4)]
        r1 = pltpu.roll(a[1], 96, 1)
        r2 = pltpu.roll(a[2], 64, 1)
        r3 = pltpu.roll(a[3], 32, 1)
        tiles = [
            jnp.where(lane < 96, a[0], r1),
            jnp.where(lane < 64, r1, r2),
            jnp.where(lane < 32, r2, r3),
        ]
        quantise(tiles, out_ref, t)
        put = pltpu.make_async_copy(out_ref.at[t], out_hbm.at[t], out_sems.at[t])
        put.start()
        puts.append(put)
    for put in puts:
        put.wait()


def prepare_kernel(lat_dev, back_ref, vert_ref, out_ref, mix_ref):
    ncells, levels = back_ref.shape
    lon_dev = ncells // lat_dev
    v_high, v_low = split(vert_ref[...].T)
    mix_ref[...] = jnp.zeros_like(mix_ref)
    mix_ref[:levels, :levels] = v_high
    mix_ref[:levels, LANES : LANES + levels] = v_low
    mix_ref[LANES : LANES + levels, :levels] = v_high
    out_ref[...] = jnp.zeros_like(out_ref)
    for lat in range(lat_dev):
        out_ref[lat * lon_dev : (lat + 1) * lon_dev, :levels] = back_ref[
            pl.ds(lat, lon_dev, stride=lat_dev), :
        ]


def toeplitz_kernel(kern_ref, ph_ref, pl_ref, mh_ref, ml_ref):
    n = kern_ref.shape[1]
    block = 256
    for high_ref, low_ref, row, sign in ((ph_ref, pl_ref, 0, False), (mh_ref, ml_ref, 1, True)):
        base = jnp.broadcast_to(kern_ref[row : row + 1, :], (block, n))
        strip = pltpu.roll(base, 0, 1, stride=1, stride_axis=0)
        for i in range(n // block):
            if i:
                strip = jnp.concatenate([strip[:, n - block :], strip[:, : n - block]], axis=1)
            piece = strip
            if sign:
                row_i = lax.broadcasted_iota(I32, (block, n), 0) + i * block
                piece = jnp.where(lax.broadcasted_iota(I32, (block, n), 1) > row_i, -strip, strip)
            high, low = split(piece)
            high_ref[i * block : (i + 1) * block, :] = high
            low_ref[i * block : (i + 1) * block, :] = low


def conv_kernel(*refs):
    got_hbm, mats, out_hbm = refs[0], refs[1:5], refs[5]
    got_ref, held, (xp, xm, yp, ym, out_ref, in_sems, mat_sems, out_sems) = (
        refs[6],
        refs[7:11],
        refs[11:],
    )
    n_lon = got_ref.shape[0]
    rows = got_ref.shape[1] - CODE_ROWS
    width = got_ref.shape[2]
    half = n_lon // 2
    gets = [
        pltpu.make_async_copy(got_hbm.at[s], got_ref.at[s], in_sems.at[s]) for s in range(n_lon)
    ]
    for s in range(half):
        gets[s].start()
        gets[s + half].start()
    loads = [pltpu.make_async_copy(a, b, mat_sems.at[i]) for i, (a, b) in enumerate(zip(mats, held))]
    for load in loads:
        load.start()
    ph_ref, pl_ref, mh_ref, ml_ref = held
    for s in range(half):
        gets[s].wait()
        gets[s + half].wait()
        a = dequantise(got_ref, s)
        b = dequantise(got_ref, s + half)
        at = slice(s * rows, (s + 1) * rows)
        xp[at, :width], xp[at, width:] = split(a + b)
        xm[at, :width], xm[at, width:] = split(a - b)
    for i, (th, tl, x, y) in enumerate(((ph_ref, pl_ref, xp, yp), (mh_ref, ml_ref, xm, ym))):
        loads[2 * i].wait()
        loads[2 * i + 1].wait()
        both = jnp.dot(th[...], x[...], preferred_element_type=F32)
        rest = jnp.dot(tl[...], x[:, :width], preferred_element_type=F32)
        y[...] = both[:, :width] + (both[:, width:] + rest)
    puts = []
    for s in range(half):
        at = slice(s * rows, (s + 1) * rows)
        plus, minus = yp[at, :], ym[at, :]
        for place, y in ((s, 0.5 * (plus + minus)), (s + half, 0.5 * (plus - minus))):
            quantise([y[:, k : k + LANES] for k in range(0, width, LANES)], out_ref, place)
            put = pltpu.make_async_copy(out_ref.at[place], out_hbm.at[place], out_sems.at[place])
            put.start()
            puts.append(put)
    for put in puts:
        put.wait()


def unpack_kernel(got_ref, out_ref, held_ref):
    lon_dev, lats, levels = out_ref.shape
    lane = lax.broadcasted_iota(I32, (lon_dev, LANES), 1)
    for t in range(got_ref.shape[0]):
        x = dequantise(got_ref, t)
        o = [x[:, k * LANES : (k + 1) * LANES] for k in range(3)]
        a = [
            o[0],
            pltpu.roll(jnp.where(lane >= 96, o[0], o[1]), 32, 1),
            pltpu.roll(jnp.where(lane >= 64, o[1], o[2]), 64, 1),
            pltpu.roll(o[2], 96, 1),
        ]
        for j in range(4):
            at = (t * 4 + j) * lon_dev
            held_ref[at : at + lon_dev, :] = a[j]
    row = lax.broadcasted_iota(I32, (8, LANES), 0)
    for i in range(0, lon_dev, 8):
        for g in range(0, lats, 8):
            square = [held_ref[(g + j) * lon_dev + i : (g + j) * lon_dev + i + 8, :] for j in range(8)]
            for n, line in enumerate(transpose8(square, row)):
                out_ref[i + n, g : g + 8, :] = line[:, :levels]


def transpose8(square, row):
    for step in (4, 2, 1):
        low = (row & step) == 0
        turned = list(square)
        for j in range(8):
            if j & step:
                continue
            a, b = square[j], square[j + step]
            turned[j] = jnp.where(low, a, pltpu.roll(b, step, 0))
            turned[j + step] = jnp.where(low, pltpu.roll(a, 8 - step, 0), b)
        square = turned
    return square


def call_spread(got, ordered, mixer, capacity, lon_dev, lat_dev, levels, coded):
    slots = got.shape[0]
    ncells = lon_dev * lat_dev
    acc = pltpu.VMEM((ncells + 8, LANES), F32)
    return pl.pallas_call(
        lambda *refs: spread_kernel(capacity, lon_dev, lat_dev, levels, *refs),
        out_shape=jax.ShapeDtypeStruct(coded, I16),
        in_specs=[pl.BlockSpec(memory_space=pl.ANY)] * 2 + vmem(1),
        out_specs=pl.BlockSpec(memory_space=pl.ANY),
        scratch_shapes=[
            pltpu.VMEM((slots, LANES), BF16),
            pltpu.VMEM(coded, I16),
            pltpu.VMEM((slots, LANES), F32),
            pltpu.VMEM((slots // 8, LANES), F32),
            pltpu.VMEM((34, 1, slots // 8), I32),
            pltpu.SemaphoreType.DMA((35,)),
            pltpu.SemaphoreType.DMA((4,)),
            pltpu.SemaphoreType.DMA((coded[0],)),
        ]
        + [acc] * N_ACC
        + [pltpu.SMEM((slots // 8,), I32)] * 34,
        compiler_params=params(),
        name="spread",
    )(got, ordered, mixer)


def call_convolve(columns, toeplitz, half, width, coded):
    part = pltpu.VMEM((half, 2 * width), BF16)
    wide = pltpu.VMEM((half, width), F32)
    n_lon = coded[0]
    anywhere = pl.BlockSpec(memory_space=pl.ANY)
    return pl.pallas_call(
        conv_kernel,
        out_shape=jax.ShapeDtypeStruct(coded, I16),
        in_specs=[anywhere] * 5,
        out_specs=anywhere,
        scratch_shapes=[pltpu.VMEM(coded, I16)]
        + [pltpu.VMEM((half, half), BF16)] * 4
        + [part] * 2
        + [wide] * 2
        + [
            pltpu.VMEM(coded, I16),
            pltpu.SemaphoreType.DMA((n_lon,)),
            pltpu.SemaphoreType.DMA((4,)),
            pltpu.SemaphoreType.DMA((n_lon,)),
        ],
        compiler_params=params(),
        name="convolve",
    )(columns, *toeplitz)


def call_unpack(back, lon_dev, lat_dev, levels, coded):
    n_lon = coded[0]
    return pl.pallas_call(
        unpack_kernel,
        grid=(n_lon // 4,),
        out_shape=jax.ShapeDtypeStruct((lon_dev, lat_dev, levels), F32),
        in_specs=[pl.BlockSpec((4,) + coded[1:], lambda g: (g, 0, 0))],
        out_specs=pl.BlockSpec((lon_dev, 16, levels), lambda g: (0, g, 0)),
        scratch_shapes=[pltpu.VMEM((16 * lon_dev, LANES), F32)],
        compiler_params=params(),
        name="unpack",
    )(back)


def per_device(
    radiances,
    owner_id,
    cell_index,
    valid_count,
    row_counts,
    jacobian,
    background,
    vertical,
    lon_kernel,
):
    n_lon = lax.axis_size("lon")
    ndev = n_lon * lax.axis_size("lat")
    nrows = radiances.shape[0]
    lon_dev, lat_dev, levels = background.shape
    capacity = 5 * nrows // (2 * ndev)
    slots = ndev * capacity
    ncells = lon_dev * lat_dev
    width = ncells // n_lon // lon_dev * levels
    coded = (n_lon, lon_dev + CODE_ROWS, width)

    sent = pl.pallas_call(
        lambda *refs: dispatch_kernel(capacity, *refs),
        out_shape=jax.ShapeDtypeStruct((slots, LANES), BF16),
        in_specs=[pl.BlockSpec(memory_space=pltpu.SMEM)] + vmem(5),
        out_specs=vmem(1)[0],
        scratch_shapes=[
            pltpu.VMEM((nrows, LANES), F32),
            pltpu.VMEM((slots + 8, LANES), F32),
            pltpu.VMEM((slots + 8, LANES), F32),
            pltpu.VMEM((1, nrows), I32),
            pltpu.SMEM((nrows,), I32),
            pltpu.SemaphoreType.DMA,
        ],
        compiler_params=params(),
        name="dispatch",
    )(
        row_counts,
        radiances,
        owner_id.T,
        cell_index.T,
        valid_count.reshape(1, nrows),
        jacobian.T,
    )
    sent, background, vertical = lax.optimization_barrier((sent, background, vertical))
    got = lax.all_to_all(
        sent.reshape(ndev, capacity, LANES), ("lon", "lat"), split_axis=0, concat_axis=0, tiled=True
    ).reshape(slots, LANES)
    ordered, mixer = pl.pallas_call(
        lambda *refs: prepare_kernel(lat_dev, *refs),
        out_shape=(
            jax.ShapeDtypeStruct((ncells, LANES), F32),
            jax.ShapeDtypeStruct((2 * LANES, 2 * LANES), BF16),
        ),
        in_specs=vmem(2),
        out_specs=tuple(vmem(2)),
        compiler_params=params(63),
        cost_estimate=pl.CostEstimate(flops=0, bytes_accessed=12_000_000, transcendentals=0),
        name="prepare",
    )(background.reshape(ncells, levels), vertical)
    field = call_spread(got, ordered, mixer, capacity, lon_dev, lat_dev, levels, coded)

    half = n_lon * lon_dev // 2
    turned_kernel = jnp.roll(lon_kernel[::-1], 1)
    plus = turned_kernel[:half] + turned_kernel[half:]
    minus = turned_kernel[half:] - turned_kernel[:half]
    first = lon_kernel[:half] - lon_kernel[half:]
    minus = jnp.roll(first[::-1], 1)
    square = jax.ShapeDtypeStruct((half, half), BF16)
    toeplitz = pl.pallas_call(
        toeplitz_kernel,
        out_shape=(square,) * 4,
        in_specs=vmem(1),
        out_specs=tuple(vmem(4)),
        compiler_params=params(63),
        name="toeplitz",
    )(jnp.stack([plus, minus]))

    columns = lax.all_to_all(field, "lon", split_axis=0, concat_axis=0, tiled=True)
    result = call_convolve(columns, toeplitz, half, width, coded)
    back = lax.all_to_all(result, "lon", split_axis=0, concat_axis=0, tiled=True)
    return call_unpack(back, lon_dev, lat_dev, levels, coded)


def solution(mesh):
    return jax.shard_map(
        per_device,
        mesh=mesh,
        in_specs=(
            P(("lon", "lat"), None),
            P(("lon", "lat"), None),
            P(("lon", "lat"), None),
            P(("lon", "lat")),
            P(("lon", "lat")),
            P(),
            P("lon", "lat", None),
            P(),
            P(),
        ),
        out_specs=P("lon", "lat", None),
        check_vma=False,
    )
```

```python
import jax
import jax.numpy as jnp
from jax import lax
from jax.experimental import pallas as pl
from jax.experimental.pallas import tpu as pltpu
from jax.sharding import PartitionSpec as P

F32 = jnp.float32
BF16 = jnp.bfloat16
I32 = jnp.int32
I16 = jnp.int16
LANES = 128
N_ACC = 8
TOP = 32700.0
LOWEST = -110.0
CODE_ROWS = 8


def vmem(n):
    return [pl.BlockSpec(memory_space=pltpu.VMEM)] * n


def params(mib=56):
    return pltpu.CompilerParams(vmem_limit_bytes=mib * 1024 * 1024)


def quantise(tiles, out_ref, place, first=0):
    rows = tiles[0].shape[0]
    for k, tile in enumerate(tiles):
        top = jnp.max(jnp.abs(tile), axis=0, keepdims=True)
        power = jnp.maximum(jnp.ceil(jnp.log2(top)), LOWEST)
        factor = jnp.exp2(-power) * TOP
        digits = jnp.round(tile * factor)
        codes = jnp.broadcast_to(power, (CODE_ROWS, LANES))
        whole = jnp.concatenate([digits, codes], axis=0).astype(I32)
        out_ref[place, :, first + k * LANES : first + (k + 1) * LANES] = whole.astype(I16)


def dequantise(in_ref, place):
    whole = in_ref[place].astype(I32).astype(F32)
    rows = whole.shape[0] - CODE_ROWS
    factor = jnp.exp2(whole[rows : rows + 1]) * (1.0 / TOP)
    return whole[:rows] * factor


def split(x):
    high = x.astype(BF16)
    low = (x - high.astype(F32)).astype(BF16)
    return high, low


def dispatch_kernel(
    capacity,
    live_ref,
    rad_ref,
    owner_ref,
    cell_ref,
    count_ref,
    jac_ref,
    out_ref,
    pay_ref,
    even_ref,
    odd_ref,
    slot_v,
    slot_s,
    sem,
):
    nrows = rad_ref.shape[0]
    levels = jac_ref.shape[0]
    slots = out_ref.shape[0]
    ndev = slots // capacity
    foot = cell_ref.shape[0]
    n_live = live_ref[0]
    block = 256
    owner_ids = lax.broadcasted_iota(I32, (ndev, block), 0)
    earlier = (
        lax.broadcasted_iota(I32, (block, block), 0) < lax.broadcasted_iota(I32, (block, block), 1)
    ).astype(F32).astype(BF16)


    def hits(b):
        cols = slice(b * block, (b + 1) * block)
        position = lax.broadcasted_iota(I32, (1, block), 1) + b * block
        live = position < n_live
        owner = owner_ref[:, cols]
        hit = (owner_ids == owner) & live
        full = count_ref[:, cols] > 2
        return live, owner, (hit & full).astype(F32), (hit & ~full).astype(F32)

    full_carry = jnp.zeros((ndev, 1), F32)
    rest_carry = full_carry
    for b in range(nrows // block):
        rest_carry = rest_carry + jnp.sum(hits(b)[2], axis=1, keepdims=True)
    for b in range(nrows // block):
        live, owner, full, rest = hits(b)
        both = jnp.concatenate([full, rest], axis=0).astype(BF16)
        before = jnp.dot(both, earlier, preferred_element_type=F32)
        rank = full * (before[:ndev] + full_carry) + rest * (before[ndev:] + rest_carry)
        rank = jnp.sum(rank, axis=0, keepdims=True).astype(I32)
        full_carry = full_carry + jnp.sum(full, axis=1, keepdims=True)
        rest_carry = rest_carry + jnp.sum(rest, axis=1, keepdims=True)
        slot = jnp.where(live, owner * capacity + rank, slots)
        for i in range(block // LANES):
            row = b * (block // LANES) + i
            slot_v[:, row * LANES : (row + 1) * LANES] = slot[:, i * LANES : (i + 1) * LANES]
    copy = pltpu.make_async_copy(slot_v.at[0], slot_s, sem)
    copy.start()
    for b in range(nrows // block):
        cols = slice(b * block, (b + 1) * block)
        profile = lax.dot_general(
            jac_ref[...], rad_ref[cols, :], (((1,), (1,)), ((), ())), preferred_element_type=F32
        )
        count = count_ref[:, cols]
        share = (profile * (1.0 / count.astype(F32))).astype(BF16).astype(F32)
        cell = cell_ref[:, cols]
        used = lax.broadcasted_iota(I32, (foot, block), 0) < count
        lon = jnp.where(used, cell // 64, 0).astype(F32)
        lat = jnp.where(used, cell % 64, 64).astype(F32)
        kind = lax.broadcasted_iota(I32, (LANES - levels - 2 * foot, block), 0)
        rest = jnp.where((kind == 0) | ((kind == 1) & (count > 2)), 1.0, 0.0)
        payload = jnp.concatenate([share, jnp.concatenate([lon, lat], axis=0), rest], axis=0)
        pay_ref[cols, :] = payload.T
    even_ref[...] = jnp.zeros_like(even_ref)
    odd_ref[...] = jnp.zeros_like(odd_ref)
    copy.wait()
    unroll = 16

    def move(c, _):
        for u in range(unroll):
            slot = slot_s[c * unroll + u]
            to_ref = odd_ref if u % 2 else even_ref
            to_ref[pl.ds(slot, 1), :] = pay_ref[pl.ds(c * unroll + u, 1), :]
        return 0

    lax.fori_loop(0, (n_live + unroll - 1) // unroll, move, 0)
    out_ref[...] = (even_ref[:slots, :] + odd_ref[:slots, :]).astype(BF16)


def spread_kernel(
    capacity,
    lon_dev,
    lat_dev,
    levels,
    got_hbm,
    back_ref,
    mix_ref,
    out_hbm,
    got_ref,
    out_ref,
    share_ref,
    fields_v,
    meta_v,
    sems,
    got_sems,
    out_sems,
    *held,
):
    accs, tables = held[:N_ACC], held[N_ACC:]
    slots = got_ref.shape[0]
    ndev = slots // capacity
    ncells = lon_dev * lat_dev
    foot = 4
    load = pltpu.make_async_copy(back_ref, accs[0].at[pl.ds(0, ncells), :], sems.at[0])
    load.start()
    n_gets = 4
    piece = slots // n_gets
    gets = []
    for i in range(n_gets):
        at = pl.ds(i * piece, piece)
        get = pltpu.make_async_copy(got_hbm.at[at, :], got_ref.at[at, :], got_sems.at[i])
        get.start()
        gets.append(get)
    for acc in accs[1:]:
        acc[...] = jnp.zeros_like(acc)
    chunk = 8
    span = foot * chunk
    row_i = lax.broadcasted_iota(I32, (LANES, LANES), 0) - levels
    lane_i = lax.broadcasted_iota(I32, (LANES, LANES), 1)
    group = lane_i // chunk
    pick = jnp.where((row_i >= 0) & (row_i <= 2 * foot) & (row_i == group), 1.0, 0.0)
    pick = jnp.where((row_i == 2 * foot + 1) & (group == 2 * foot), 8.0, pick).astype(BF16)
    block = 256
    own = lax.broadcasted_iota(I32, (block, LANES), 0) % chunk
    own = own == lax.broadcasted_iota(I32, (block, LANES), 1) % chunk
    chunk_i = lax.broadcasted_iota(I32, (block // chunk, block), 0)
    gather = chunk_i == lax.broadcasted_iota(I32, (block // chunk, block), 1) // chunk
    gather = jnp.where(gather, 1.0, 0.0).astype(BF16)
    is_cell = lax.broadcasted_iota(I32, (block // chunk, LANES), 1) < span
    for b in range(slots // block):
        if b * block % piece == 0:
            gets[b * block // piece].wait()
        rows = slice(b * block, (b + 1) * block)
        part = got_ref[rows, :]
        fields = jnp.dot(part, pick, preferred_element_type=F32)
        fields = jnp.where(own, fields, 0.0).astype(BF16)
        table = jnp.dot(gather, fields, preferred_element_type=F32)
        turned = pltpu.roll(table, LANES - span, 1)
        table = jnp.where(is_cell, table + turned * float(lon_dev), table)
        at = b * (block // chunk)
        fields_v[at : at + block // chunk, :] = table
    lanes = list(range(span)) + [2 * span]
    for i in range(slots // chunk // LANES):
        cols = slice(i * LANES, (i + 1) * LANES)
        turned = fields_v[cols, :].T.astype(I32)
        for k, lane in enumerate(lanes):
            meta_v[k, :, cols] = turned[lane : lane + 1, :]
    copies = [pltpu.make_async_copy(meta_v.at[k, 0], t, sems.at[k + 1]) for k, t in enumerate(tables)]
    for copy in copies:
        copy.start()
    share_ref[...] = got_ref[...].astype(F32)
    load.wait()
    for copy in copies:
        copy.wait()
    per_source = capacity // chunk

    def one_source(s, _):
        base = s * per_source
        code = tables[span][base]
        for c in range(1, per_source):
            code = code + tables[span][base + c]
        n_chunks, n_full = code & 7, code >> 3

        def one_chunk(c, used):
            first = pl.multiple_of(c * chunk, chunk)
            for u in range(chunk):
                row = share_ref[pl.ds(first + u, 1), :]
                for f in range(used):
                    cell = tables[f * chunk + u][c]
                    acc = accs[(u * used + f) % N_ACC]
                    acc[pl.ds(cell, 1), :] = acc[pl.ds(cell, 1), :] + row

        def full_chunk(c, _):
            one_chunk(c, foot)
            return 0

        def half_chunk(c, _):
            one_chunk(c, foot // 2)
            return 0

        lax.fori_loop(base, base + n_full, full_chunk, 0)
        lax.fori_loop(base + n_full, base + n_chunks, half_chunk, 0)
        return 0

    lax.fori_loop(0, ndev, one_source, 0)
    lane = lax.broadcasted_iota(I32, (lon_dev, LANES), 1)

    puts = []
    for t in range(ncells // (4 * lon_dev)):
        rows = pl.ds(t * 4 * lon_dev, 4 * lon_dev)
        sums = [acc[rows, :] for acc in accs]
        while len(sums) > 1:
            sums = [a + b for a, b in zip(sums[::2], sums[1::2])]
        total = sums[0]
        high, low = split(total)
        both = jnp.dot(
            jnp.concatenate([high, low], axis=1), mix_ref[...], preferred_element_type=F32
        )
        mixed = both[:, :LANES] + both[:, LANES:]
        a = [mixed[j * lon_dev : (j + 1) * lon_dev, :] for j in range(4)]
        r1 = pltpu.roll(a[1], 96, 1)
        r2 = pltpu.roll(a[2], 64, 1)
        r3 = pltpu.roll(a[3], 32, 1)
        tiles = [
            jnp.where(lane < 96, a[0], r1),
            jnp.where(lane < 64, r1, r2),
            jnp.where(lane < 32, r2, r3),
        ]
        quantise(tiles, out_ref, t)
        put = pltpu.make_async_copy(out_ref.at[t], out_hbm.at[t], out_sems.at[t])
        put.start()
        puts.append(put)
    for put in puts:
        put.wait()


def prepare_kernel(lat_dev, back_ref, vert_ref, out_ref, mix_ref):
    ncells, levels = back_ref.shape
    lon_dev = ncells // lat_dev
    v_high, v_low = split(vert_ref[...].T)
    mix_ref[...] = jnp.zeros_like(mix_ref)
    mix_ref[:levels, :levels] = v_high
    mix_ref[:levels, LANES : LANES + levels] = v_low
    mix_ref[LANES : LANES + levels, :levels] = v_high
    out_ref[...] = jnp.zeros_like(out_ref)
    for lat in range(lat_dev):
        out_ref[lat * lon_dev : (lat + 1) * lon_dev, :levels] = back_ref[
            pl.ds(lat, lon_dev, stride=lat_dev), :
        ]


def toeplitz_kernel(kern_ref, ph_ref, pl_ref, mh_ref, ml_ref):
    n = kern_ref.shape[1]
    block = 256
    for high_ref, low_ref, row, sign in ((ph_ref, pl_ref, 0, False), (mh_ref, ml_ref, 1, True)):
        base = jnp.broadcast_to(kern_ref[row : row + 1, :], (block, n))
        strip = pltpu.roll(base, 0, 1, stride=1, stride_axis=0)
        for i in range(n // block):
            if i:
                strip = jnp.concatenate([strip[:, n - block :], strip[:, : n - block]], axis=1)
            piece = strip
            if sign:
                row_i = lax.broadcasted_iota(I32, (block, n), 0) + i * block
                piece = jnp.where(lax.broadcasted_iota(I32, (block, n), 1) > row_i, -strip, strip)
            high, low = split(piece)
            high_ref[i * block : (i + 1) * block, :] = high
            low_ref[i * block : (i + 1) * block, :] = low


def conv_kernel(*refs):
    got_hbm, mats, out_hbm = refs[0], refs[1:5], refs[5]
    got_ref, held, (xp, xm, yp, ym, out_ref, in_sems, mat_sems, out_sems) = (
        refs[6],
        refs[7:11],
        refs[11:],
    )
    n_lon = got_ref.shape[0]
    rows = got_ref.shape[1] - CODE_ROWS
    width = got_ref.shape[2]
    half = n_lon // 2
    parts = ((0, 2 * LANES), (2 * LANES, width))
    gets = [
        pltpu.make_async_copy(got_hbm.at[s], got_ref.at[s], in_sems.at[s]) for s in range(n_lon)
    ]
    for s in range(half):
        gets[s].start()
        gets[s + half].start()
    loads = [pltpu.make_async_copy(a, b, mat_sems.at[i]) for i, (a, b) in enumerate(zip(mats, held))]
    for load in loads:
        load.start()
    ph_ref, pl_ref, mh_ref, ml_ref = held
    for s in range(half):
        gets[s].wait()
        gets[s + half].wait()
        a = dequantise(got_ref, s)
        b = dequantise(got_ref, s + half)
        at = slice(s * rows, (s + 1) * rows)
        for x, value in ((xp, a + b), (xm, a - b)):
            high, low = split(value)
            for begin, end in parts:
                x[at, 2 * begin : begin + end] = high[:, begin:end]
                x[at, begin + end : 2 * end] = low[:, begin:end]
    puts = []
    for begin, end in parts:
        wide = end - begin
        for i, (th, tl, x, y) in enumerate(((ph_ref, pl_ref, xp, yp), (mh_ref, ml_ref, xm, ym))):
            if begin == 0:
                loads[2 * i].wait()
                loads[2 * i + 1].wait()
            both = jnp.dot(th[...], x[:, 2 * begin : 2 * end], preferred_element_type=F32)
            rest = jnp.dot(tl[...], x[:, 2 * begin : begin + end], preferred_element_type=F32)
            y[:, begin:end] = both[:, :wide] + (both[:, wide:] + rest)
        for s in range(half):
            at = slice(s * rows, (s + 1) * rows)
            plus, minus = yp[at, begin:end], ym[at, begin:end]
            for place, y in ((s, 0.5 * (plus + minus)), (s + half, 0.5 * (plus - minus))):
                tiles = [y[:, k : k + LANES] for k in range(0, wide, LANES)]
                quantise(tiles, out_ref, place, begin)
                if end == width:
                    put = pltpu.make_async_copy(
                        out_ref.at[place], out_hbm.at[place], out_sems.at[place]
                    )
                    put.start()
                    puts.append(put)
    for put in puts:
        put.wait()


def unpack_kernel(got_ref, out_ref, held_ref):
    lon_dev, lats, levels = out_ref.shape
    lane = lax.broadcasted_iota(I32, (lon_dev, LANES), 1)
    for t in range(got_ref.shape[0]):
        x = dequantise(got_ref, t)
        o = [x[:, k * LANES : (k + 1) * LANES] for k in range(3)]
        a = [
            o[0],
            pltpu.roll(jnp.where(lane >= 96, o[0], o[1]), 32, 1),
            pltpu.roll(jnp.where(lane >= 64, o[1], o[2]), 64, 1),
            pltpu.roll(o[2], 96, 1),
        ]
        for j in range(4):
            at = (t * 4 + j) * lon_dev
            held_ref[at : at + lon_dev, :] = a[j]
    row = lax.broadcasted_iota(I32, (8, LANES), 0)
    for i in range(0, lon_dev, 8):
        for g in range(0, lats, 8):
            square = [held_ref[(g + j) * lon_dev + i : (g + j) * lon_dev + i + 8, :] for j in range(8)]
            for n, line in enumerate(transpose8(square, row)):
                out_ref[i + n, g : g + 8, :] = line[:, :levels]


def transpose8(square, row):
    for step in (4, 2, 1):
        low = (row & step) == 0
        turned = list(square)
        for j in range(8):
            if j & step:
                continue
            a, b = square[j], square[j + step]
            turned[j] = jnp.where(low, a, pltpu.roll(b, step, 0))
            turned[j + step] = jnp.where(low, pltpu.roll(a, 8 - step, 0), b)
        square = turned
    return square


def call_spread(got, ordered, mixer, capacity, lon_dev, lat_dev, levels, coded):
    slots = got.shape[0]
    ncells = lon_dev * lat_dev
    acc = pltpu.VMEM((ncells + 8, LANES), F32)
    return pl.pallas_call(
        lambda *refs: spread_kernel(capacity, lon_dev, lat_dev, levels, *refs),
        out_shape=jax.ShapeDtypeStruct(coded, I16),
        in_specs=[pl.BlockSpec(memory_space=pl.ANY)] * 2 + vmem(1),
        out_specs=pl.BlockSpec(memory_space=pl.ANY),
        scratch_shapes=[
            pltpu.VMEM((slots, LANES), BF16),
            pltpu.VMEM(coded, I16),
            pltpu.VMEM((slots, LANES), F32),
            pltpu.VMEM((slots // 8, LANES), F32),
            pltpu.VMEM((33, 1, slots // 8), I32),
            pltpu.SemaphoreType.DMA((34,)),
            pltpu.SemaphoreType.DMA((4,)),
            pltpu.SemaphoreType.DMA((coded[0],)),
        ]
        + [acc] * N_ACC
        + [pltpu.SMEM((slots // 8,), I32)] * 33,
        compiler_params=params(),
        name="spread",
    )(got, ordered, mixer)


def call_convolve(columns, toeplitz, half, width, coded):
    part = pltpu.VMEM((half, 2 * width), BF16)
    wide = pltpu.VMEM((half, width), F32)
    n_lon = coded[0]
    anywhere = pl.BlockSpec(memory_space=pl.ANY)
    return pl.pallas_call(
        conv_kernel,
        out_shape=jax.ShapeDtypeStruct(coded, I16),
        in_specs=[anywhere] * 5,
        out_specs=anywhere,
        scratch_shapes=[pltpu.VMEM(coded, I16)]
        + [pltpu.VMEM((half, half), BF16)] * 4
        + [part] * 2
        + [wide] * 2
        + [
            pltpu.VMEM(coded, I16),
            pltpu.SemaphoreType.DMA((n_lon,)),
            pltpu.SemaphoreType.DMA((4,)),
            pltpu.SemaphoreType.DMA((n_lon,)),
        ],
        compiler_params=params(),
        name="convolve",
    )(columns, *toeplitz)


def call_unpack(back, lon_dev, lat_dev, levels, coded):
    n_lon = coded[0]
    return pl.pallas_call(
        unpack_kernel,
        grid=(n_lon // 4,),
        out_shape=jax.ShapeDtypeStruct((lon_dev, lat_dev, levels), F32),
        in_specs=[pl.BlockSpec((4,) + coded[1:], lambda g: (g, 0, 0))],
        out_specs=pl.BlockSpec((lon_dev, 16, levels), lambda g: (0, g, 0)),
        scratch_shapes=[pltpu.VMEM((16 * lon_dev, LANES), F32)],
        compiler_params=params(),
        name="unpack",
    )(back)


def per_device(
    radiances,
    owner_id,
    cell_index,
    valid_count,
    row_counts,
    jacobian,
    background,
    vertical,
    lon_kernel,
):
    n_lon = lax.axis_size("lon")
    ndev = n_lon * lax.axis_size("lat")
    nrows = radiances.shape[0]
    lon_dev, lat_dev, levels = background.shape
    capacity = 5 * nrows // (2 * ndev)
    slots = ndev * capacity
    ncells = lon_dev * lat_dev
    width = ncells // n_lon // lon_dev * levels
    coded = (n_lon, lon_dev + CODE_ROWS, width)

    sent = pl.pallas_call(
        lambda *refs: dispatch_kernel(capacity, *refs),
        out_shape=jax.ShapeDtypeStruct((slots, LANES), BF16),
        in_specs=[pl.BlockSpec(memory_space=pltpu.SMEM)] + vmem(5),
        out_specs=vmem(1)[0],
        scratch_shapes=[
            pltpu.VMEM((nrows, LANES), F32),
            pltpu.VMEM((slots + 8, LANES), F32),
            pltpu.VMEM((slots + 8, LANES), F32),
            pltpu.VMEM((1, nrows), I32),
            pltpu.SMEM((nrows,), I32),
            pltpu.SemaphoreType.DMA,
        ],
        compiler_params=params(),
        name="dispatch",
    )(
        row_counts,
        radiances,
        owner_id.T,
        cell_index.T,
        valid_count.reshape(1, nrows),
        jacobian.T,
    )
    sent, background, vertical = lax.optimization_barrier((sent, background, vertical))
    got = lax.all_to_all(
        sent.reshape(ndev, capacity, LANES), ("lon", "lat"), split_axis=0, concat_axis=0, tiled=True
    ).reshape(slots, LANES)
    ordered, mixer = pl.pallas_call(
        lambda *refs: prepare_kernel(lat_dev, *refs),
        out_shape=(
            jax.ShapeDtypeStruct((ncells, LANES), F32),
            jax.ShapeDtypeStruct((2 * LANES, 2 * LANES), BF16),
        ),
        in_specs=vmem(2),
        out_specs=tuple(vmem(2)),
        compiler_params=params(63),
        cost_estimate=pl.CostEstimate(flops=0, bytes_accessed=12_000_000, transcendentals=0),
        name="prepare",
    )(background.reshape(ncells, levels), vertical)
    field = call_spread(got, ordered, mixer, capacity, lon_dev, lat_dev, levels, coded)

    half = n_lon * lon_dev // 2
    turned_kernel = jnp.roll(lon_kernel[::-1], 1)
    plus = turned_kernel[:half] + turned_kernel[half:]
    minus = turned_kernel[half:] - turned_kernel[:half]
    first = lon_kernel[:half] - lon_kernel[half:]
    minus = jnp.roll(first[::-1], 1)
    square = jax.ShapeDtypeStruct((half, half), BF16)
    toeplitz = pl.pallas_call(
        toeplitz_kernel,
        out_shape=(square,) * 4,
        in_specs=vmem(1),
        out_specs=tuple(vmem(4)),
        compiler_params=params(63),
        name="toeplitz",
    )(jnp.stack([plus, minus]))

    columns = lax.all_to_all(field, "lon", split_axis=0, concat_axis=0, tiled=True)
    result = call_convolve(columns, toeplitz, half, width, coded)
    back = lax.all_to_all(result, "lon", split_axis=0, concat_axis=0, tiled=True)
    return call_unpack(back, lon_dev, lat_dev, levels, coded)


def solution(mesh):
    return jax.shard_map(
        per_device,
        mesh=mesh,
        in_specs=(
            P(("lon", "lat"), None),
            P(("lon", "lat"), None),
            P(("lon", "lat"), None),
            P(("lon", "lat")),
            P(("lon", "lat")),
            P(),
            P("lon", "lat", None),
            P(),
            P(),
        ),
        out_specs=P("lon", "lat", None),
        check_vma=False,
    )
```

```python
import jax
import jax.numpy as jnp
from jax import lax
from jax.experimental import pallas as pl
from jax.experimental.pallas import tpu as pltpu
from jax.sharding import PartitionSpec as P

F32 = jnp.float32
BF16 = jnp.bfloat16
I32 = jnp.int32
I16 = jnp.int16
LANES = 128
N_ACC = 8
TOP = 32700.0
LOWEST = -110.0
CODE_ROWS = 8


def vmem(n):
    return [pl.BlockSpec(memory_space=pltpu.VMEM)] * n


def params(mib=56):
    return pltpu.CompilerParams(vmem_limit_bytes=mib * 1024 * 1024)


def quantise(tiles, out_ref, place):
    rows = tiles[0].shape[0]
    for k, tile in enumerate(tiles):
        top = jnp.max(jnp.abs(tile), axis=0, keepdims=True)
        power = jnp.maximum(jnp.ceil(jnp.log2(top)), LOWEST)
        factor = jnp.exp2(-power) * TOP
        digits = jnp.round(tile * factor)
        codes = jnp.broadcast_to(power, (CODE_ROWS, LANES))
        whole = jnp.concatenate([digits, codes], axis=0).astype(I32)
        out_ref[place, :, k * LANES : (k + 1) * LANES] = whole.astype(I16)


def dequantise(in_ref, place):
    whole = in_ref[place].astype(I32).astype(F32)
    rows = whole.shape[0] - CODE_ROWS
    factor = jnp.exp2(whole[rows : rows + 1]) * (1.0 / TOP)
    return whole[:rows] * factor


def split(x):
    high = x.astype(BF16)
    low = (x - high.astype(F32)).astype(BF16)
    return high, low


def dispatch_kernel(
    capacity,
    live_ref,
    rad_ref,
    owner_ref,
    cell_ref,
    count_ref,
    jac_ref,
    out_ref,
    pay_ref,
    even_ref,
    odd_ref,
    slot_v,
    slot_s,
    sem,
):
    nrows = rad_ref.shape[0]
    levels = jac_ref.shape[0]
    slots = out_ref.shape[0]
    ndev = slots // capacity
    foot = cell_ref.shape[0]
    n_live = live_ref[0]
    block = 256
    owner_ids = lax.broadcasted_iota(I32, (ndev, block), 0)
    earlier = (
        lax.broadcasted_iota(I32, (block, block), 0) < lax.broadcasted_iota(I32, (block, block), 1)
    ).astype(F32).astype(BF16)


    def hits(b):
        cols = slice(b * block, (b + 1) * block)
        position = lax.broadcasted_iota(I32, (1, block), 1) + b * block
        live = position < n_live
        owner = owner_ref[:, cols]
        hit = (owner_ids == owner) & live
        full = count_ref[:, cols] > 2
        return live, owner, (hit & full).astype(F32), (hit & ~full).astype(F32)

    full_carry = jnp.zeros((ndev, 1), F32)
    rest_carry = full_carry
    for b in range(nrows // block):
        rest_carry = rest_carry + jnp.sum(hits(b)[2], axis=1, keepdims=True)
    for b in range(nrows // block):
        live, owner, full, rest = hits(b)
        both = jnp.concatenate([full, rest], axis=0).astype(BF16)
        before = jnp.dot(both, earlier, preferred_element_type=F32)
        rank = full * (before[:ndev] + full_carry) + rest * (before[ndev:] + rest_carry)
        rank = jnp.sum(rank, axis=0, keepdims=True).astype(I32)
        full_carry = full_carry + jnp.sum(full, axis=1, keepdims=True)
        rest_carry = rest_carry + jnp.sum(rest, axis=1, keepdims=True)
        slot = jnp.where(live, owner * capacity + rank, slots)
        for i in range(block // LANES):
            row = b * (block // LANES) + i
            slot_v[:, row * LANES : (row + 1) * LANES] = slot[:, i * LANES : (i + 1) * LANES]
    copy = pltpu.make_async_copy(slot_v.at[0], slot_s, sem)
    copy.start()
    for b in range(nrows // block):
        cols = slice(b * block, (b + 1) * block)
        profile = lax.dot_general(
            jac_ref[...], rad_ref[cols, :], (((1,), (1,)), ((), ())), preferred_element_type=F32
        )
        count = count_ref[:, cols]
        share = (profile * (1.0 / count.astype(F32))).astype(BF16).astype(F32)
        cell = cell_ref[:, cols]
        used = lax.broadcasted_iota(I32, (foot, block), 0) < count
        lon = jnp.where(used, cell // 64, 0).astype(F32)
        lat = jnp.where(used, cell % 64, 64).astype(F32)
        kind = lax.broadcasted_iota(I32, (LANES - levels - 2 * foot, block), 0)
        rest = jnp.where((kind == 0) | ((kind == 1) & (count > 2)), 1.0, 0.0)
        payload = jnp.concatenate([share, jnp.concatenate([lon, lat], axis=0), rest], axis=0)
        pay_ref[cols, :] = payload.T
    even_ref[...] = jnp.zeros_like(even_ref)
    odd_ref[...] = jnp.zeros_like(odd_ref)
    copy.wait()
    unroll = 16

    def move(c, _):
        for u in range(unroll):
            slot = slot_s[c * unroll + u]
            to_ref = odd_ref if u % 2 else even_ref
            to_ref[pl.ds(slot, 1), :] = pay_ref[pl.ds(c * unroll + u, 1), :]
        return 0

    lax.fori_loop(0, (n_live + unroll - 1) // unroll, move, 0)
    out_ref[...] = (even_ref[:slots, :] + odd_ref[:slots, :]).astype(BF16)


def spread_kernel(
    capacity,
    lon_dev,
    lat_dev,
    levels,
    got_hbm,
    back_ref,
    mix_ref,
    out_hbm,
    got_ref,
    out_ref,
    share_ref,
    fields_v,
    meta_v,
    sems,
    got_sems,
    out_sems,
    *held,
):
    accs, tables = held[:N_ACC], held[N_ACC:]
    slots = got_ref.shape[0]
    ndev = slots // capacity
    ncells = lon_dev * lat_dev
    foot = 4
    load = pltpu.make_async_copy(back_ref, accs[0].at[pl.ds(0, ncells), :], sems.at[0])
    load.start()
    n_gets = 4
    piece = slots // n_gets
    gets = []
    for i in range(n_gets):
        at = pl.ds(i * piece, piece)
        get = pltpu.make_async_copy(got_hbm.at[at, :], got_ref.at[at, :], got_sems.at[i])
        get.start()
        gets.append(get)
    for acc in accs[1:]:
        acc[...] = jnp.zeros_like(acc)
    chunk = 8
    span = foot * chunk
    row_i = lax.broadcasted_iota(I32, (LANES, LANES), 0) - levels
    lane_i = lax.broadcasted_iota(I32, (LANES, LANES), 1)
    group = lane_i // chunk
    pick = jnp.where((row_i >= 0) & (row_i <= 2 * foot) & (row_i == group), 1.0, 0.0)
    pick = jnp.where((row_i == 2 * foot + 1) & (group == 2 * foot), 8.0, pick).astype(BF16)
    block = 256
    own = lax.broadcasted_iota(I32, (block, LANES), 0) % chunk
    own = own == lax.broadcasted_iota(I32, (block, LANES), 1) % chunk
    chunk_i = lax.broadcasted_iota(I32, (block // chunk, block), 0)
    gather = chunk_i == lax.broadcasted_iota(I32, (block // chunk, block), 1) // chunk
    gather = jnp.where(gather, 1.0, 0.0).astype(BF16)
    is_cell = lax.broadcasted_iota(I32, (block // chunk, LANES), 1) < span
    for b in range(slots // block):
        if b * block % piece == 0:
            gets[b * block // piece].wait()
        rows = slice(b * block, (b + 1) * block)
        part = got_ref[rows, :]
        fields = jnp.dot(part, pick, preferred_element_type=F32)
        fields = jnp.where(own, fields, 0.0).astype(BF16)
        table = jnp.dot(gather, fields, preferred_element_type=F32)
        turned = pltpu.roll(table, LANES - span, 1)
        table = jnp.where(is_cell, table + turned * float(lon_dev), table)
        at = b * (block // chunk)
        fields_v[at : at + block // chunk, :] = table
    lanes = list(range(span)) + [2 * span]
    for i in range(slots // chunk // LANES):
        cols = slice(i * LANES, (i + 1) * LANES)
        turned = fields_v[cols, :].T.astype(I32)
        for k, lane in enumerate(lanes):
            meta_v[k, :, cols] = turned[lane : lane + 1, :]
    copies = [pltpu.make_async_copy(meta_v.at[k, 0], t, sems.at[k + 1]) for k, t in enumerate(tables)]
    for copy in copies:
        copy.start()
    share_ref[...] = got_ref[...].astype(F32)
    load.wait()
    for copy in copies:
        copy.wait()
    per_source = capacity // chunk

    def one_source(s, _):
        base = s * per_source
        code = tables[span][base]
        for c in range(1, per_source):
            code = code + tables[span][base + c]
        n_chunks, n_full = code & 7, code >> 3

        def one_chunk(c, used):
            first = pl.multiple_of(c * chunk, chunk)
            for u in range(chunk):
                row = share_ref[pl.ds(first + u, 1), :]
                for f in range(used):
                    cell = tables[f * chunk + u][c]
                    acc = accs[(u * used + f) % N_ACC]
                    acc[pl.ds(cell, 1), :] = acc[pl.ds(cell, 1), :] + row

        def full_chunk(c, _):
            one_chunk(c, foot)
            return 0

        def half_chunk(c, _):
            one_chunk(c, foot // 2)
            return 0

        lax.fori_loop(base, base + n_full, full_chunk, 0)
        lax.fori_loop(base + n_full, base + n_chunks, half_chunk, 0)
        return 0

    lax.fori_loop(0, ndev, one_source, 0)
    lane = lax.broadcasted_iota(I32, (lon_dev, LANES), 1)

    puts = []
    for t in range(ncells // (4 * lon_dev)):
        rows = pl.ds(t * 4 * lon_dev, 4 * lon_dev)
        sums = [acc[rows, :] for acc in accs]
        while len(sums) > 1:
            sums = [a + b for a, b in zip(sums[::2], sums[1::2])]
        total = sums[0]
        high, low = split(total)
        both = jnp.dot(
            jnp.concatenate([high, low], axis=1), mix_ref[...], preferred_element_type=F32
        )
        mixed = both[:, :LANES] + both[:, LANES:]
        a = [mixed[j * lon_dev : (j + 1) * lon_dev, :] for j in range(4)]
        r1 = pltpu.roll(a[1], 96, 1)
        r2 = pltpu.roll(a[2], 64, 1)
        r3 = pltpu.roll(a[3], 32, 1)
        tiles = [
            jnp.where(lane < 96, a[0], r1),
            jnp.where(lane < 64, r1, r2),
            jnp.where(lane < 32, r2, r3),
        ]
        quantise(tiles, out_ref, t)
        put = pltpu.make_async_copy(out_ref.at[t], out_hbm.at[t], out_sems.at[t])
        put.start()
        puts.append(put)
    for put in puts:
        put.wait()


def prepare_kernel(lat_dev, back_ref, vert_ref, out_ref, mix_ref):
    ncells, levels = back_ref.shape
    lon_dev = ncells // lat_dev
    v_high, v_low = split(vert_ref[...].T)
    mix_ref[...] = jnp.zeros_like(mix_ref)
    mix_ref[:levels, :levels] = v_high
    mix_ref[:levels, LANES : LANES + levels] = v_low
    mix_ref[LANES : LANES + levels, :levels] = v_high
    out_ref[...] = jnp.zeros_like(out_ref)
    for lat in range(lat_dev):
        out_ref[lat * lon_dev : (lat + 1) * lon_dev, :levels] = back_ref[
            pl.ds(lat, lon_dev, stride=lat_dev), :
        ]


def toeplitz_kernel(kern_ref, ph_ref, pl_ref, mh_ref, ml_ref):
    n = kern_ref.shape[1]
    block = 256
    for high_ref, low_ref, row, sign in ((ph_ref, pl_ref, 0, False), (mh_ref, ml_ref, 1, True)):
        base = jnp.broadcast_to(kern_ref[row : row + 1, :], (block, n))
        strip = pltpu.roll(base, 0, 1, stride=1, stride_axis=0)
        for i in range(n // block):
            if i:
                strip = jnp.concatenate([strip[:, n - block :], strip[:, : n - block]], axis=1)
            piece = strip
            if sign:
                row_i = lax.broadcasted_iota(I32, (block, n), 0) + i * block
                piece = jnp.where(lax.broadcasted_iota(I32, (block, n), 1) > row_i, -strip, strip)
            high, low = split(piece)
            high_ref[i * block : (i + 1) * block, :] = high
            low_ref[i * block : (i + 1) * block, :] = low


def conv_kernel(*refs):
    got_hbm, mats, out_hbm = refs[0], refs[1:5], refs[5]
    got_ref, held, (xp, xm, yp, ym, out_ref, in_sems, mat_sems, out_sems) = (
        refs[6],
        refs[7:11],
        refs[11:],
    )
    n_lon = got_ref.shape[0]
    rows = got_ref.shape[1] - CODE_ROWS
    width = got_ref.shape[2]
    half = n_lon // 2
    gets = [
        pltpu.make_async_copy(got_hbm.at[s], got_ref.at[s], in_sems.at[s]) for s in range(n_lon)
    ]
    for s in range(half):
        gets[s].start()
        gets[s + half].start()
    loads = [pltpu.make_async_copy(a, b, mat_sems.at[i]) for i, (a, b) in enumerate(zip(mats, held))]
    for load in loads:
        load.start()
    ph_ref, pl_ref, mh_ref, ml_ref = held
    for s in range(half):
        gets[s].wait()
        gets[s + half].wait()
        a = dequantise(got_ref, s)
        b = dequantise(got_ref, s + half)
        at = slice(s * rows, (s + 1) * rows)
        xp[at, :width], xp[at, width:] = split(a + b)
        xm[at, :width], xm[at, width:] = split(a - b)
    for i, (th, tl, x, y) in enumerate(((ph_ref, pl_ref, xp, yp), (mh_ref, ml_ref, xm, ym))):
        loads[2 * i].wait()
        loads[2 * i + 1].wait()
        both = jnp.dot(th[...], x[...], preferred_element_type=F32)
        rest = jnp.dot(tl[...], x[:, :width], preferred_element_type=F32)
        y[...] = both[:, :width] + (both[:, width:] + rest)
    puts = []
    for s in range(half):
        at = slice(s * rows, (s + 1) * rows)
        plus, minus = yp[at, :], ym[at, :]
        for place, y in ((s, 0.5 * (plus + minus)), (s + half, 0.5 * (plus - minus))):
            quantise([y[:, k : k + LANES] for k in range(0, width, LANES)], out_ref, place)
            put = pltpu.make_async_copy(out_ref.at[place], out_hbm.at[place], out_sems.at[place])
            put.start()
            puts.append(put)
    for put in puts:
        put.wait()


def unpack_kernel(got_ref, out_ref, held_ref):
    lon_dev, lats, levels = out_ref.shape
    lane = lax.broadcasted_iota(I32, (lon_dev, LANES), 1)
    for t in range(got_ref.shape[0]):
        x = dequantise(got_ref, t)
        o = [x[:, k * LANES : (k + 1) * LANES] for k in range(3)]
        a = [
            o[0],
            pltpu.roll(jnp.where(lane >= 96, o[0], o[1]), 32, 1),
            pltpu.roll(jnp.where(lane >= 64, o[1], o[2]), 64, 1),
            pltpu.roll(o[2], 96, 1),
        ]
        for j in range(4):
            at = (t * 4 + j) * lon_dev
            held_ref[at : at + lon_dev, :] = a[j]
    row = lax.broadcasted_iota(I32, (8, LANES), 0)
    for i in range(0, lon_dev, 8):
        for g in range(0, lats, 8):
            square = [held_ref[(g + j) * lon_dev + i : (g + j) * lon_dev + i + 8, :] for j in range(8)]
            for n, line in enumerate(transpose8(square, row)):
                out_ref[i + n, g : g + 8, :] = line[:, :levels]


def transpose8(square, row):
    for step in (4, 2, 1):
        low = (row & step) == 0
        turned = list(square)
        for j in range(8):
            if j & step:
                continue
            a, b = square[j], square[j + step]
            turned[j] = jnp.where(low, a, pltpu.roll(b, step, 0))
            turned[j + step] = jnp.where(low, pltpu.roll(a, 8 - step, 0), b)
        square = turned
    return square


def call_spread(got, ordered, mixer, capacity, lon_dev, lat_dev, levels, coded):
    slots = got.shape[0]
    ncells = lon_dev * lat_dev
    acc = pltpu.VMEM((ncells + 8, LANES), F32)
    return pl.pallas_call(
        lambda *refs: spread_kernel(capacity, lon_dev, lat_dev, levels, *refs),
        out_shape=jax.ShapeDtypeStruct(coded, I16),
        in_specs=[pl.BlockSpec(memory_space=pl.ANY)] * 2 + vmem(1),
        out_specs=pl.BlockSpec(memory_space=pl.ANY),
        scratch_shapes=[
            pltpu.VMEM((slots, LANES), BF16),
            pltpu.VMEM(coded, I16),
            pltpu.VMEM((slots, LANES), F32),
            pltpu.VMEM((slots // 8, LANES), F32),
            pltpu.VMEM((33, 1, slots // 8), I32),
            pltpu.SemaphoreType.DMA((34,)),
            pltpu.SemaphoreType.DMA((4,)),
            pltpu.SemaphoreType.DMA((coded[0],)),
        ]
        + [acc] * N_ACC
        + [pltpu.SMEM((slots // 8,), I32)] * 33,
        compiler_params=params(),
        name="spread",
    )(got, ordered, mixer)


def call_convolve(columns, toeplitz, half, width, coded):
    part = pltpu.VMEM((half, 2 * width), BF16)
    wide = pltpu.VMEM((half, width), F32)
    n_lon = coded[0]
    anywhere = pl.BlockSpec(memory_space=pl.ANY)
    return pl.pallas_call(
        conv_kernel,
        out_shape=jax.ShapeDtypeStruct(coded, I16),
        in_specs=[anywhere] * 5,
        out_specs=anywhere,
        scratch_shapes=[pltpu.VMEM(coded, I16)]
        + [pltpu.VMEM((half, half), BF16)] * 4
        + [part] * 2
        + [wide] * 2
        + [
            pltpu.VMEM(coded, I16),
            pltpu.SemaphoreType.DMA((n_lon,)),
            pltpu.SemaphoreType.DMA((4,)),
            pltpu.SemaphoreType.DMA((n_lon,)),
        ],
        compiler_params=params(),
        name="convolve",
    )(columns, *toeplitz)


def call_unpack(back, lon_dev, lat_dev, levels, coded):
    n_lon = coded[0]
    return pl.pallas_call(
        unpack_kernel,
        grid=(n_lon // 4,),
        out_shape=jax.ShapeDtypeStruct((lon_dev, lat_dev, levels), F32),
        in_specs=[pl.BlockSpec((4,) + coded[1:], lambda g: (g, 0, 0))],
        out_specs=pl.BlockSpec((lon_dev, 16, levels), lambda g: (0, g, 0)),
        scratch_shapes=[pltpu.VMEM((16 * lon_dev, LANES), F32)],
        compiler_params=params(),
        name="unpack",
    )(back)


def per_device(
    radiances,
    owner_id,
    cell_index,
    valid_count,
    row_counts,
    jacobian,
    background,
    vertical,
    lon_kernel,
):
    n_lon = lax.axis_size("lon")
    ndev = n_lon * lax.axis_size("lat")
    nrows = radiances.shape[0]
    lon_dev, lat_dev, levels = background.shape
    capacity = 5 * nrows // (2 * ndev)
    slots = ndev * capacity
    ncells = lon_dev * lat_dev
    width = ncells // n_lon // lon_dev * levels
    coded = (n_lon, lon_dev + CODE_ROWS, width)

    sent = pl.pallas_call(
        lambda *refs: dispatch_kernel(capacity, *refs),
        out_shape=jax.ShapeDtypeStruct((slots, LANES), BF16),
        in_specs=[pl.BlockSpec(memory_space=pltpu.SMEM)] + vmem(5),
        out_specs=vmem(1)[0],
        scratch_shapes=[
            pltpu.VMEM((nrows, LANES), F32),
            pltpu.VMEM((slots + 8, LANES), F32),
            pltpu.VMEM((slots + 8, LANES), F32),
            pltpu.VMEM((1, nrows), I32),
            pltpu.SMEM((nrows,), I32),
            pltpu.SemaphoreType.DMA,
        ],
        compiler_params=params(),
        name="dispatch",
    )(
        row_counts,
        radiances,
        owner_id.T,
        cell_index.T,
        valid_count.reshape(1, nrows),
        jacobian.T,
    )
    sent, background, vertical = lax.optimization_barrier((sent, background, vertical))
    got = lax.all_to_all(
        sent.reshape(ndev, capacity, LANES), ("lon", "lat"), split_axis=0, concat_axis=0, tiled=True
    ).reshape(slots, LANES)
    ordered, mixer = pl.pallas_call(
        lambda *refs: prepare_kernel(lat_dev, *refs),
        out_shape=(
            jax.ShapeDtypeStruct((ncells, LANES), F32),
            jax.ShapeDtypeStruct((2 * LANES, 2 * LANES), BF16),
        ),
        in_specs=vmem(2),
        out_specs=tuple(vmem(2)),
        compiler_params=params(63),
        cost_estimate=pl.CostEstimate(flops=0, bytes_accessed=12_000_000, transcendentals=0),
        name="prepare",
    )(background.reshape(ncells, levels), vertical)
    field = call_spread(got, ordered, mixer, capacity, lon_dev, lat_dev, levels, coded)

    half = n_lon * lon_dev // 2
    turned_kernel = jnp.roll(lon_kernel[::-1], 1)
    plus = turned_kernel[:half] + turned_kernel[half:]
    minus = turned_kernel[half:] - turned_kernel[:half]
    first = lon_kernel[:half] - lon_kernel[half:]
    minus = jnp.roll(first[::-1], 1)
    square = jax.ShapeDtypeStruct((half, half), BF16)
    toeplitz = pl.pallas_call(
        toeplitz_kernel,
        out_shape=(square,) * 4,
        in_specs=vmem(1),
        out_specs=tuple(vmem(4)),
        compiler_params=params(63),
        name="toeplitz",
    )(jnp.stack([plus, minus]))

    columns = lax.all_to_all(field, "lon", split_axis=0, concat_axis=0, tiled=True)
    result = call_convolve(columns, toeplitz, half, width, coded)
    back = lax.all_to_all(result, "lon", split_axis=0, concat_axis=0, tiled=True)
    return call_unpack(back, lon_dev, lat_dev, levels, coded)


def solution(mesh):
    return jax.shard_map(
        per_device,
        mesh=mesh,
        in_specs=(
            P(("lon", "lat"), None),
            P(("lon", "lat"), None),
            P(("lon", "lat"), None),
            P(("lon", "lat")),
            P(("lon", "lat")),
            P(),
            P("lon", "lat", None),
            P(),
            P(),
        ),
        out_specs=P("lon", "lat", None),
        check_vma=False,
    )
```
